128 devices in a mesh: section: 4 (over y), ctx: 32 (over x, z, core).
Axes of the slice: x: 4, y: 4, z: 4, core: 2. Of those that a mesh axis runs over, the one named last changes fastest.
Arguments:
- tokens: bfloat16 [4, 16384, 3072], P('section', 'ctx'), may hold values from -3 to 3
- queries: bfloat16 [4, 16384, 1536], P('section', 'ctx'), may hold values from -36 to 36
- keyvals: bfloat16 [4, 16384, 2, 1536], P('section', 'ctx'), may hold values from -9 to 9
- out_weight: bfloat16 [4, 1536, 3072], P('section'), may hold values from -0.15625 to 0.15625
- gate: float32 [4, 3072], P('section'), may hold values from 0.5 to 2
- cube_order: int32 [4, 32, 512], P('section', 'ctx'), may hold values from 0 to 511, as said below
- crit_owner: int32 [4, 256, 12], P('section', 'ctx'), may hold values from 0 to 31, as said below
- crit_tile: int32 [4, 256, 12], P('section', 'ctx'), may hold values from 0 to 7, as said below
- crit_count: int32 [4, 256], P('section', 'ctx'), may hold values from 6 to 12
Outputs:
- handed: bfloat16 [4, 16384, 3072], P('section', 'ctx')
The draws below stay inside these ranges and needn't reach their ends.
Inputs may be any that keep to these rules, and one draw needn't show every extreme that they name: `crit_owner`: entry 0 of each list is the query tile itself (its own ctx index and tile). Within the first crit_count entries no tile repeats and entries 1 onward name tiles of other ctx indices; later entries repeat the query tile itself. Over the live entries of the 8 lists of one ctx index, at most 2 distinct tiles of any other ctx index are named; in every section one ctx index is asked for 2 tiles by every other one. `crit_tile`: tile numbers within their holder. Each row cube_order[s, d] is a permutation of 0 to 511.
All inputs are finite; a program needn't handle non-finite values.
Results may differ from the reference program's by a relative error of at most 0.0042.
Values may be sent and summed in bfloat16 or wider, within the bound.
A program may use at most 192 MiB of HBM per device.

```python
import math
import jax
import jax.numpy as jnp
from jax import lax

D = 3072
HEADS = 12
HEAD_DIM = 128
TILE = 64
LIST = 12
QT_DEV = 8
HW = 1536
TOK_DEV = 512
SECTIONS = 4
QTILES = 256
TOKENS = 16384
N_CTX = 32


def cube_rows_draw(key):
    key = jax.random.fold_in(key, 41)
    ctx_ranks = QTILES // QT_DEV
    noise = jax.random.randint(key, (SECTIONS, ctx_ranks, TOK_DEV), 0, 2 ** 18)
    ranked = noise * TOK_DEV + jnp.arange(TOK_DEV, dtype=jnp.int32)
    return jnp.argsort(ranked, axis=-1, stable=True).astype(jnp.int32)


def list_draw(key):
    ctx_ranks = QTILES // QT_DEV
    pool_size = 2 * ctx_ranks
    key_first = jax.random.fold_in(key, 60)
    key_second = jax.random.fold_in(key, 61)
    key_hot = jax.random.fold_in(key, 62)
    key_score = jax.random.fold_in(key, 63)
    key_count = jax.random.fold_in(key, 64)
    first = jax.random.randint(key_first, (SECTIONS, ctx_ranks, ctx_ranks), 0, QT_DEV)
    second = (first + jax.random.randint(key_second, (SECTIONS, ctx_ranks, ctx_ranks), 1, QT_DEV)) % QT_DEV
    hot_owner = jax.random.randint(key_hot, (SECTIONS,), 0, ctx_ranks)
    pool_index = jnp.arange(pool_size, dtype=jnp.int32)
    pool_owner = pool_index // 2
    pool_tile = jnp.where(pool_index % 2 == 0, first[:, :, pool_owner], second[:, :, pool_owner])
    noise = jax.random.randint(key_score, (SECTIONS, ctx_ranks, QT_DEV, pool_size), 0, 2 ** 20)
    ranked = noise * pool_size + pool_index
    requester = jnp.arange(ctx_ranks, dtype=jnp.int32)[None, :, None, None]
    query_tile = jnp.arange(QT_DEV, dtype=jnp.int32)[None, None, :, None]
    favoured = (pool_owner[None, None, None, :] == hot_owner[:, None, None, None]) & (query_tile == 1)
    ranked = jnp.where(favoured, ranked + 2 ** 28, ranked)
    ranked = jnp.where(pool_owner[None, None, None, :] == requester, -1, ranked)
    picked = lax.top_k(ranked, LIST - 1)[1]
    pick_owner = pool_owner[picked]
    pick_tile = jnp.take_along_axis(jnp.broadcast_to(pool_tile[:, :, None, :], ranked.shape), picked, axis=-1)
    lead_shape = (SECTIONS, ctx_ranks, QT_DEV, 1)
    owners = jnp.concatenate([jnp.broadcast_to(requester, lead_shape), pick_owner], axis=-1)
    tile_ids = jnp.concatenate([jnp.broadcast_to(query_tile, lead_shape), pick_tile], axis=-1)
    counts = jax.random.randint(key_count, (SECTIONS, ctx_ranks, QT_DEV), LIST // 2, LIST + 1)
    counts = jnp.where(query_tile[..., 0] < 2, LIST, counts)
    is_live = jnp.arange(LIST, dtype=jnp.int32)[None, None, None, :] < counts[..., None]
    owners = jnp.where(is_live, owners, requester)
    tile_ids = jnp.where(is_live, tile_ids, query_tile)
    return (owners.reshape(SECTIONS, QTILES, LIST).astype(jnp.int32), tile_ids.reshape(SECTIONS, QTILES, LIST).astype(jnp.int32), counts.reshape(SECTIONS, QTILES).astype(jnp.int32))


def draw_queries(key, part):
    key = jax.random.fold_in(key, 5)
    values = jnp.clip(1.5 * jax.random.normal(key, (SECTIONS, TOKENS, HW), jnp.float32), -9.0, 9.0)
    return values.astype(jnp.bfloat16)


def draw_keyvals(key, part):
    key = jax.random.fold_in(key, 9)
    values = jnp.clip(1.5 * jax.random.normal(key, (SECTIONS, TOKENS, 2, HW), jnp.float32), -9.0, 9.0)
    return values.astype(jnp.bfloat16)


def draw_cube_order(key, part):
    return cube_rows_draw(key)


def draw_crit_owner(key, part):
    return list_draw(key)[0]


def draw_crit_tile(key, part):
    return list_draw(key)[1]


def draw_crit_count(key, part):
    return list_draw(key)[2]


def block_levels(stream_key, dims, shards, least, high):
    def one(dim, shards_of):
        heights = jax.random.uniform(jax.random.fold_in(jax.random.fold_in(stream_key, 6), dim), (shards_of,), jnp.float32, least / len(shards), high / len(shards))
        return jnp.repeat(jnp.exp(heights), dims[dim] // shards_of).reshape((-1,) + (1,) * (len(dims) - dim - 1))

    factor_of = one(*shards[0])
    for cut in shards[1:]:
        factor_of = factor_of * one(*cut)
    return factor_of


def centred(stream_key, extent, spread, bound, shards=(), held_as=jnp.bfloat16):
    drawn = jax.random.normal(stream_key, extent, jnp.float32) * spread
    if len(shards) > 0:
        drawn = block_levels(stream_key, extent, shards, -0.22, 0.18) * drawn
    return jnp.clip(drawn, min=-bound, max=bound).astype(held_as)


def setup_inputs(seed: int = 0) -> dict:
    key_list = jax.random.split(jax.random.key(seed), 10)
    return {
        "tokens": centred(key_list[0], (SECTIONS, TOKENS, D), 0.5, 3.0, ((0, 4), (1, 32))),
        "queries": draw_queries(jax.random.fold_in(key_list[9], 71), 0),
        "keyvals": draw_keyvals(jax.random.fold_in(key_list[9], 71), 0),
        "out_weight": centred(key_list[3], (SECTIONS, HW, D), HW ** -0.5, 0.15625, ((0, 4),)),
        "gate": jnp.clip(0.5 + 1.5 * jax.random.uniform(key_list[4], (SECTIONS, D), jnp.float32) ** block_levels(key_list[4], (SECTIONS, D), ((0, 4),), -0.2, 0.2), 0.5, 2.0),
        "cube_order": draw_cube_order(jax.random.fold_in(key_list[9], 71), 0),
        "crit_owner": draw_crit_owner(jax.random.fold_in(key_list[9], 71), 0),
        "crit_tile": draw_crit_tile(jax.random.fold_in(key_list[9], 71), 0),
        "crit_count": draw_crit_count(jax.random.fold_in(key_list[9], 71), 0),
    }


def attend_tiles(query_tiles, gathered, counts):
    blocks = query_tiles.shape[0]
    query_heads = query_tiles.reshape(blocks, TILE, HEADS, HEAD_DIM).astype(jnp.float32)
    key_heads = gathered[:, :, :, 0].reshape(blocks, LIST * TILE, HEADS, HEAD_DIM).astype(jnp.float32)
    value_heads = gathered[:, :, :, 1].reshape(blocks, LIST * TILE, HEADS, HEAD_DIM).astype(jnp.float32)
    scores = jnp.einsum('bthd,bkhd->bhtk', query_heads, key_heads) * (1.0 / math.sqrt(HEAD_DIM))
    is_live = (jnp.arange(LIST * TILE) // TILE)[None, :] < counts[:, None]
    scores = jnp.where(is_live[:, None, None, :], scores, -jnp.inf)
    row_max = lax.optimization_barrier(jnp.max(scores, axis=-1, keepdims=True))
    probable = jnp.exp(scores - row_max)
    totals = lax.optimization_barrier(jnp.sum(probable, axis=-1))
    weights = lax.optimization_barrier(probable.astype(jnp.bfloat16)).astype(jnp.float32)
    blended = jnp.einsum('bhtk,bkhd->bthd', weights, value_heads)
    blended = blended / jnp.transpose(totals, (0, 2, 1))[..., None]
    return blended.reshape(blocks, TILE, HW).astype(jnp.bfloat16)

def block_section(tokens, queries, keyvals, out_weight, gate, cube_rows, owners, tile_ids, counts):
    query_blocks = queries.reshape(N_CTX, TOK_DEV, HW)
    pair_blocks = keyvals.reshape(N_CTX, TOK_DEV, 2, HW)
    cube_query = jnp.take_along_axis(query_blocks, cube_rows[:, :, None], axis=1)
    cube_pairs = jnp.take_along_axis(pair_blocks, cube_rows[:, :, None, None], axis=1)
    all_tiles = cube_pairs.reshape(QTILES, TILE, 2, HW)
    listed = (owners * QT_DEV + tile_ids).reshape(N_CTX, QT_DEV, LIST)

    def one_device(pieces):
        query_dev, listed_dev, count_dev = pieces
        gathered = jnp.take(all_tiles, listed_dev.reshape(-1), axis=0).reshape(QT_DEV, LIST, TILE, 2, HW)
        return attend_tiles(query_dev.reshape(QT_DEV, TILE, HW), gathered, count_dev)
    outputs = lax.map(one_device, (cube_query, listed, counts.reshape(N_CTX, QT_DEV)))
    cube_out = outputs.reshape(N_CTX, TOK_DEV, HW)
    raster = jnp.zeros_like(cube_out).at[jnp.arange(N_CTX)[:, None], cube_rows].set(cube_out)
    projected = jnp.dot(raster.reshape(TOKENS, HW), out_weight, preferred_element_type=jnp.float32)
    return (tokens.astype(jnp.float32) + gate[None, :] * projected).astype(jnp.bfloat16)

def reference(tokens, queries, keyvals, out_weight, gate, cube_order, crit_owner, crit_tile, crit_count):
    results = []
    for section_index in range(SECTIONS):
        results.append(block_section(tokens[section_index], queries[section_index], keyvals[section_index], out_weight[section_index], gate[section_index], cube_order[section_index], crit_owner[section_index], crit_tile[section_index], crit_count[section_index]))
    stacked = jnp.stack(results)
    return jnp.roll(stacked, 1, axis=0)
```

```python
import math

import jax
import jax.numpy as jnp
from jax import lax
from jax.experimental import pallas as pl
from jax.experimental.pallas import tpu as pltpu
from jax.sharding import PartitionSpec as P

D = 3072
HEADS = 12
HEAD_DIM = 128
TILE = 64
LIST = 12
QT = 8
HW = 1536
ROWS = 512
CTX = 32
SIDE = 4
CHIPS = 16
SECTIONS = 4
KV_TILES = CTX * 2 * QT
JT = 2
CHUNK = JT * TILE
NCH = QT // JT
UNROLL = 4
NCOL = 512
EXP_SCALE = math.log2(math.e) / math.sqrt(HEAD_DIM)


def kernel(
    tok_hbm, q_hbm, kv_hbm, w_hbm, gate_ref, order_ref, codes_ref, out_hbm,
    tok, q_in, kv_in, w, perm, tok_cube, kv_stage, q_stage, kvbuf, qbuf, obuf, ones,
    orecv, ystage, yrecv, prev_order, out_stage,
    load_sem, ksend, krecv, fsend, frecv, qsend, qrecv,
    osend, orecv_sem, ysend, yrecv_sem, psend, precv, out_sem,
):
    sec = lax.axis_index("section")
    me = lax.axis_index("ctx")
    core = me % 2
    chip = me // 2
    cx, cz = chip // SIDE, chip % SIDE
    kind = (cz - cx + 3) % SIDE
    has_head = kind < 3
    head = cx + SIDE * kind
    sibling = (sec, me + 1 - 2 * core)
    ahead = ((sec + 1) % SECTIONS, me)
    behind = ((sec + SECTIONS - 1) % SECTIONS, me)

    def remote(src, dst, send, recv, device):
        return pltpu.make_async_remote_copy(
            src_ref=src, dst_ref=dst, send_sem=send, recv_sem=recv,
            device_id=device, device_id_type=pl.DeviceIdType.MESH,
        )

    def load(i):
        src = (kv_hbm, q_hbm, tok_hbm, w_hbm)[i]
        return pltpu.make_async_copy(src, (kv_in, q_in, tok, w)[i], load_sem.at[i])

    for i in range(4):
        load(i).start()

    barrier = pltpu.get_barrier_semaphore()

    def greet(i, _):
        other = (chip + i) % CHIPS
        pl.semaphore_signal(barrier, inc=1, device_id=(sec, 2 * other + core),
                            device_id_type=pl.DeviceIdType.MESH)
        return 0

    lax.fori_loop(1, CHIPS, greet, 0)
    for device in (sibling, ahead, behind):
        pl.semaphore_signal(barrier, inc=1, device_id=device,
                            device_id_type=pl.DeviceIdType.MESH)

    column = jnp.transpose(jnp.broadcast_to(order_ref[0:1, :], (128, ROWS)))[:, :1]
    perm[...] = (lax.broadcasted_iota(jnp.int32, (ROWS, ROWS), 1) == column).astype(jnp.bfloat16)
    ones[0] = jnp.ones((TILE, HEAD_DIM), jnp.bfloat16)
    ones[1] = jnp.zeros((TILE, HEAD_DIM), jnp.bfloat16)
    kvbuf[KV_TILES] = jnp.zeros((TILE, HEAD_DIM), jnp.bfloat16)

    pl.semaphore_wait(barrier, CHIPS + 2)

    def order_copy():
        return remote(order_ref, prev_order, psend, precv, ahead)

    order_copy().start()

    def target(i):
        tx, tz = (cx + i // SIDE) % SIDE, (cz + i % SIDE) % SIDE
        tkind = (tz - tx + 3) % SIDE
        return tx * SIDE + tz, tkind < 3, tx + SIDE * tkind

    def origin(i):
        return ((cx + SIDE - i // SIDE) % SIDE) * SIDE + (cz + SIDE - i % SIDE) % SIDE

    def block(ref, index, rows):
        return ref.at[pl.ds(pl.multiple_of(index * rows, rows), rows)]

    def kv_copy(i):
        to, _, thead = target(i)
        return remote(kv_stage.at[thead], block(kvbuf, me, 2 * QT), ksend.at[thead],
                      krecv.at[chip], (sec, 2 * to + core))

    def q_copy(i):
        to, _, thead = target(i)
        return remote(q_stage.at[thead], block(qbuf, chip, ROWS), qsend.at[thead],
                      qrecv.at[chip], (sec, 2 * to + core))

    def forward(from_chip):
        part = block(kvbuf, 2 * from_chip + core, 2 * QT)
        return remote(part, part, fsend.at[from_chip], frecv.at[from_chip], sibling)

    def lanes(h):
        return pl.ds(pl.multiple_of(h * HEAD_DIM, HEAD_DIM), HEAD_DIM)

    def cube_pairs(h):
        both = jnp.concatenate([kv_in[:, 0, lanes(h)], kv_in[:, 1, lanes(h)]], axis=1)
        rows = jnp.dot(perm[...], both, preferred_element_type=jnp.float32).astype(jnp.bfloat16)
        rows = rows.reshape(QT, TILE, 2 * HEAD_DIM)
        return rows[:, :, :HEAD_DIM], rows[:, :, HEAD_DIM:]

    def cube_query(h):
        return jnp.dot(perm[...], q_in[:, lanes(h)],
                       preferred_element_type=jnp.float32).astype(jnp.bfloat16)

    load(0).wait()

    def send_kv(i, _):
        _, valid, thead = target(i)

        @pl.when(valid)
        def _():
            keys, values = cube_pairs(thead)
            kv_stage[thead, 0:QT] = keys
            kv_stage[thead, QT:] = values
            kv_copy(i).start()

        return 0

    lax.fori_loop(1, CHIPS, send_kv, 0)

    @pl.when(has_head)
    def _():
        keys, values = cube_pairs(head)
        kvbuf[pl.ds(me * 2 * QT, QT)] = keys
        kvbuf[pl.ds(me * 2 * QT + QT, QT)] = values
        forward(chip).start()

    load(1).wait()

    def send_q(i, _):
        _, valid, thead = target(i)

        @pl.when(valid)
        def _():
            q_stage[thead] = cube_query(thead)
            q_copy(i).start()

        return 0

    lax.fori_loop(1, CHIPS, send_q, 0)

    @pl.when(has_head)
    def _():
        qbuf[pl.ds(pl.multiple_of(chip * ROWS, ROWS), ROWS)] = cube_query(head)

    load(2).wait()

    def cube_tokens(n, _):
        cols = pl.ds(pl.multiple_of(n * NCOL, NCOL), NCOL)
        tok_cube[:, cols] = jnp.dot(perm[...], tok[:, cols],
                                    preferred_element_type=jnp.float32).astype(jnp.bfloat16)
        return 0

    lax.fori_loop(0, D // NCOL, cube_tokens, 0)

    @pl.when(has_head)
    def _():
        def pass_on(i, _):
            src = origin(i)
            remote(kv_stage.at[0], block(kvbuf, 2 * src + core, 2 * QT), ksend.at[0],
                   krecv.at[src], sibling).wait_recv()
            forward(src).start()
            return 0

        lax.fori_loop(1, CHIPS, pass_on, 0)

        def small(i, _):
            src = origin(i)
            remote(q_stage.at[0], block(qbuf, src, ROWS), qsend.at[0], qrecv.at[src],
                   sibling).wait_recv()
            return 0

        lax.fori_loop(1, CHIPS, small, 0)

        def passed(src, _):
            part = block(kvbuf, 2 * src + 1 - core, 2 * QT)
            remote(part, part, fsend.at[src], frecv.at[src], sibling).wait_recv()
            return 0

        lax.fori_loop(0, CHIPS, passed, 0)

    load(3).wait()

    def o_rows(src, j):
        return pl.ds(pl.multiple_of(src * ROWS + j * TILE, TILE), TILE)

    def attend(src, j):
        q = qbuf[o_rows(src, j), :]
        row = (2 * src + core) * QT + j
        ks, vs, marks = [], [], []
        for e in range(LIST):
            ks.append(kvbuf[codes_ref[row, e]])
            vs.append(kvbuf[codes_ref[row, 16 + e]])
            marks.append(ones[codes_ref[row, 32 + e]])
        scores = lax.dot_general(q, jnp.concatenate(ks, 0), (((1,), (1,)), ((), ())),
                                 preferred_element_type=jnp.float32)
        top = jnp.max(scores, axis=-1, keepdims=True)
        weights = jnp.exp2((scores - top) * EXP_SCALE).astype(jnp.bfloat16)
        sums = jnp.concatenate([jnp.concatenate(vs, 0), jnp.concatenate(marks, 0)], 1)
        both = jnp.dot(weights, sums, preferred_element_type=jnp.float32)
        obuf[o_rows(src, j), :] = (both[:, :HEAD_DIM] / both[:, HEAD_DIM:]).astype(jnp.bfloat16)

    def send_o(src, j):
        part = obuf.at[o_rows(src, j)]
        place = orecv.at[head, pl.ds(pl.multiple_of(j * TILE, TILE), TILE)]
        sem = orecv_sem.at[j * HEADS + head]

        @pl.when(src != chip)
        def _():
            remote(part, place, osend.at[src], sem, (sec, 2 * src + core)).start()

        @pl.when(src == chip)
        def _():
            pltpu.make_async_copy(part, place, sem).start()

    def y_copy(ch):
        rows = pl.ds(pl.multiple_of(ch * CHUNK, CHUNK), CHUNK)
        return remote(ystage.at[rows], yrecv.at[rows], ysend.at[ch], yrecv_sem.at[ch], ahead)

    def chunk_step(ch, _):
        @pl.when(has_head & (ch < NCH))
        def _():
            def group(g, _):
                j = ch * JT + g // (CHIPS // UNROLL)
                first = chip + 1 + (g % (CHIPS // UNROLL)) * UNROLL
                for u in range(UNROLL):
                    attend((first + u) % CHIPS, j)
                for u in range(UNROLL):
                    send_o((first + u) % CHIPS, j)
                return 0

            lax.fori_loop(0, JT * CHIPS // UNROLL, group, 0)

        @pl.when(ch >= 1)
        def _():
            done = ch - 1

            def arrived(k, _):
                j = done * JT + k // HEADS
                h = k % HEADS
                place = orecv.at[h, pl.ds(pl.multiple_of(j * TILE, TILE), TILE)]
                pltpu.make_async_copy(obuf.at[pl.ds(0, TILE)], place,
                                      orecv_sem.at[j * HEADS + h]).wait()
                return 0

            lax.fori_loop(0, JT * HEADS, arrived, 0)
            rows = pl.ds(pl.multiple_of(done * CHUNK, CHUNK), CHUNK)
            attended = jnp.concatenate([orecv[h, rows, :] for h in range(HEADS)], axis=1)

            def project(n, _):
                cols = pl.ds(pl.multiple_of(n * NCOL, NCOL), NCOL)
                acc = jnp.dot(attended, w[:, cols], preferred_element_type=jnp.float32)
                ystage[rows, cols] = (
                    tok_cube[rows, cols].astype(jnp.float32) + gate_ref[0:1, cols] * acc
                ).astype(jnp.bfloat16)
                return 0

            lax.fori_loop(0, D // NCOL, project, 0)
            y_copy(done).start()

        return 0

    lax.fori_loop(0, NCH + 1, chunk_step, 0)

    order_copy().wait()
    perm[...] = (
        lax.broadcasted_iota(jnp.int32, (ROWS, ROWS), 0) == prev_order[0:1, :]
    ).astype(jnp.bfloat16)

    def y_wait(ch, _):
        y_copy(ch).wait()
        return 0

    lax.fori_loop(0, NCH, y_wait, 0)

    def out_copy(n):
        cols = pl.ds(pl.multiple_of(n * NCOL, NCOL), NCOL)
        return pltpu.make_async_copy(out_stage.at[:, cols], out_hbm.at[:, cols], out_sem.at[n])

    def restore(n, _):
        cols = pl.ds(pl.multiple_of(n * NCOL, NCOL), NCOL)
        out_stage[:, cols] = jnp.dot(perm[...], yrecv[:, cols],
                                     preferred_element_type=jnp.float32).astype(jnp.bfloat16)
        out_copy(n).start()
        return 0

    lax.fori_loop(0, D // NCOL, restore, 0)

    def drain(i, _):
        _, valid, _ = target(i)

        @pl.when(valid)
        def _():
            kv_copy(i).wait_send()
            q_copy(i).wait_send()

        return 0

    lax.fori_loop(1, CHIPS, drain, 0)

    @pl.when(has_head)
    def _():
        def drain_head(src, _):
            forward(src).wait_send()

            @pl.when(src != chip)
            def _():
                part = block(obuf, src, ROWS)
                remote(part, part, osend.at[src], orecv_sem.at[0], sibling).wait_send()

            return 0

        lax.fori_loop(0, CHIPS, drain_head, 0)

    def out_wait(n, _):
        out_copy(n).wait()
        return 0

    lax.fori_loop(0, D // NCOL, out_wait, 0)


def body(tokens, queries, keyvals, out_weight, gate, cube_order, crit_owner, crit_tile, crit_count):
    live = jnp.arange(LIST, dtype=jnp.int32)[None, :] < crit_count[0][:, None]
    k_at = crit_owner[0] * (2 * QT) + crit_tile[0]
    v_at = jnp.where(live, k_at + QT, KV_TILES)
    m_at = jnp.where(live, 0, 1)

    def wide(part):
        return jnp.pad(part, ((0, 0), (0, 16 - LIST)))

    codes = jnp.concatenate([wide(k_at), wide(v_at), wide(m_at)], axis=1)
    codes = jnp.pad(codes, ((0, 0), (0, 128 - codes.shape[1])))
    codes = lax.all_gather(codes, "ctx", axis=0, tiled=True)
    order = jnp.broadcast_to(cube_order[0], (8, ROWS))
    bf16, i32 = jnp.bfloat16, jnp.int32
    dma = pltpu.SemaphoreType.DMA
    handed = pl.pallas_call(
        kernel,
        out_shape=jax.ShapeDtypeStruct((ROWS, D), bf16),
        in_specs=[pl.BlockSpec(memory_space=pl.ANY)] * 4
        + [pl.BlockSpec(memory_space=pltpu.VMEM)] * 2
        + [pl.BlockSpec(memory_space=pltpu.SMEM)],
        out_specs=pl.BlockSpec(memory_space=pl.ANY),
        scratch_shapes=[
            pltpu.VMEM((ROWS, D), bf16),
            pltpu.VMEM((ROWS, HW), bf16),
            pltpu.VMEM((ROWS, 2, HW), bf16),
            pltpu.VMEM((HW, D), bf16),
            pltpu.VMEM((ROWS, ROWS), bf16),
            pltpu.VMEM((ROWS, D), bf16),
            pltpu.VMEM((HEADS, 2 * QT, TILE, HEAD_DIM), bf16),
            pltpu.VMEM((HEADS, ROWS, HEAD_DIM), bf16),
            pltpu.VMEM((KV_TILES + 1, TILE, HEAD_DIM), bf16),
            pltpu.VMEM((CHIPS * ROWS, HEAD_DIM), bf16),
            pltpu.VMEM((CHIPS * ROWS, HEAD_DIM), bf16),
            pltpu.VMEM((2, TILE, HEAD_DIM), bf16),
            pltpu.VMEM((HEADS, ROWS, HEAD_DIM), bf16),
            pltpu.VMEM((ROWS, D), bf16),
            pltpu.VMEM((ROWS, D), bf16),
            pltpu.VMEM((8, ROWS), i32),
            pltpu.VMEM((ROWS, D), bf16),
            dma((4,)), dma((HEADS,)), dma((CHIPS,)), dma((CHIPS,)), dma((CHIPS,)),
            dma((HEADS,)), dma((CHIPS,)),
            dma((CHIPS,)), dma((QT * HEADS,)), dma((NCH,)), dma((NCH,)), dma, dma,
            dma((D // NCOL,)),
        ],
        compiler_params=pltpu.CompilerParams(
            collective_id=0, has_side_effects=True, vmem_limit_bytes=60 * 2**20
        ),
        cost_estimate=pl.CostEstimate(
            flops=16 * 10**9, bytes_accessed=22 * 2**20, transcendentals=10**7
        ),
        name="cube_attention",
    )(tokens[0], queries[0], keyvals[0], out_weight[0], gate, order, codes)
    return handed[None]


def solution(mesh):
    in_specs = (
        P("section", "ctx", None),
        P("section", "ctx", None),
        P("section", "ctx", None, None),
        P("section", None, None),
        P("section", None),
        P("section", "ctx", None),
        P("section", "ctx", None),
        P("section", "ctx", None),
        P("section", "ctx"),
    )
    out_specs = P("section", "ctx", None)
    return jax.shard_map(body, mesh=mesh, in_specs=in_specs, out_specs=out_specs, check_vma=False)
```

```python
import math

import jax
import jax.numpy as jnp
from jax import lax
from jax.experimental import pallas as pl
from jax.experimental.pallas import tpu as pltpu
from jax.sharding import PartitionSpec as P

D = 3072
HEADS = 12
HEAD_DIM = 128
TILE = 64
LIST = 12
QT = 8
HW = 1536
ROWS = 512
CTX = 32
SIDE = 4
CHIPS = 16
SECTIONS = 4
KV_TILES = CTX * 2 * QT
JT = 1
CHUNK = JT * TILE
NCH = QT // JT
UNROLL = 4
NCOL = 512
EXP_SCALE = math.log2(math.e) / math.sqrt(HEAD_DIM)


def kernel(
    tok_hbm, q_hbm, kv_hbm, w_hbm, gate_ref, order_ref, codes_ref, yrecv, prev_order,
    tok, q_in, kv_in, w, perm, tok_cube, kv_stage, q_stage, kvbuf, qbuf, obuf, ones,
    lists, lists_smem, orecv, ystage,
    load_sem, smem_sem, ksend, krecv, fsend, frecv, qsend, qrecv, lsend, lrecv,
    osend, orecv_sem, ysend, yrecv_sem, psend, precv,
):
    sec = lax.axis_index("section")
    me = lax.axis_index("ctx")
    core = me % 2
    chip = me // 2
    cx, cz = chip // SIDE, chip % SIDE
    kind = (cz - cx + 3) % SIDE
    has_head = kind < 3
    head = cx + SIDE * kind
    sibling = (sec, me + 1 - 2 * core)
    ahead = ((sec + 1) % SECTIONS, me)
    behind = ((sec + SECTIONS - 1) % SECTIONS, me)

    def remote(src, dst, send, recv, device):
        return pltpu.make_async_remote_copy(
            src_ref=src, dst_ref=dst, send_sem=send, recv_sem=recv,
            device_id=device, device_id_type=pl.DeviceIdType.MESH,
        )

    def load(i):
        src = (kv_hbm, q_hbm, tok_hbm, w_hbm)[i]
        return pltpu.make_async_copy(src, (kv_in, q_in, tok, w)[i], load_sem.at[i])

    for i in range(4):
        load(i).start()

    barrier = pltpu.get_barrier_semaphore()

    def greet(i, _):
        other = (chip + i) % CHIPS
        pl.semaphore_signal(barrier, inc=1, device_id=(sec, 2 * other + core),
                            device_id_type=pl.DeviceIdType.MESH)
        return 0

    lax.fori_loop(1, CHIPS, greet, 0)
    for device in (sibling, ahead, behind):
        pl.semaphore_signal(barrier, inc=1, device_id=device,
                            device_id_type=pl.DeviceIdType.MESH)

    column = jnp.transpose(jnp.broadcast_to(order_ref[...], (128, ROWS)))[:, :1]
    perm[...] = (lax.broadcasted_iota(jnp.int32, (ROWS, ROWS), 1) == column).astype(jnp.bfloat16)
    ones[0] = jnp.ones((TILE, HEAD_DIM), jnp.bfloat16)
    ones[1] = jnp.zeros((TILE, HEAD_DIM), jnp.bfloat16)
    kvbuf[KV_TILES] = jnp.zeros((TILE, HEAD_DIM), jnp.bfloat16)

    pl.semaphore_wait(barrier, CHIPS + 2)

    def order_copy():
        return remote(order_ref, prev_order, psend, precv, ahead)

    order_copy().start()

    def shift(i):
        return i % SIDE, (i // SIDE + 3 * (i % SIDE)) % SIDE

    def target(i):
        dx, dz = shift(i)
        tx, tz = (cx + dx) % SIDE, (cz + dz) % SIDE
        tkind = (tz - tx + 3) % SIDE
        return tx * SIDE + tz, tkind < 3, tx + SIDE * tkind

    def origin(i):
        dx, dz = shift(i)
        return ((cx + SIDE - dx) % SIDE) * SIDE + (cz + SIDE - dz) % SIDE

    def block(ref, index, rows):
        return ref.at[pl.ds(pl.multiple_of(index * rows, rows), rows)]

    def list_copy(i):
        to, _, thead = target(i)
        return remote(codes_ref, block(lists, chip, QT), lsend.at[thead], lrecv.at[chip],
                      (sec, 2 * to + core))

    def kv_copy(i):
        to, _, thead = target(i)
        return remote(kv_stage.at[thead], block(kvbuf, me, 2 * QT), ksend.at[thead],
                      krecv.at[chip], (sec, 2 * to + core))

    def q_rows(src, ch):
        return pl.ds(pl.multiple_of(src * ROWS + ch * CHUNK, CHUNK), CHUNK)

    def q_copy(i, ch):
        to, _, thead = target(i)
        rows = pl.ds(pl.multiple_of(ch * CHUNK, CHUNK), CHUNK)
        return remote(q_stage.at[thead, rows], qbuf.at[q_rows(chip, ch)], qsend.at[thead],
                      qrecv.at[chip * NCH + ch], (sec, 2 * to + core))

    def forward(from_chip):
        part = block(kvbuf, 2 * from_chip + core, 2 * QT)
        return remote(part, part, fsend.at[from_chip], frecv.at[from_chip], sibling)

    def lanes(h):
        return pl.ds(pl.multiple_of(h * HEAD_DIM, HEAD_DIM), HEAD_DIM)

    def cube_pairs(h):
        both = jnp.concatenate([kv_in[:, 0, lanes(h)], kv_in[:, 1, lanes(h)]], axis=1)
        rows = jnp.dot(perm[...], both, preferred_element_type=jnp.float32).astype(jnp.bfloat16)
        rows = rows.reshape(QT, TILE, 2 * HEAD_DIM)
        return rows[:, :, :HEAD_DIM], rows[:, :, HEAD_DIM:]

    def cube_query(h):
        return jnp.dot(perm[...], q_in[:, lanes(h)],
                       preferred_element_type=jnp.float32).astype(jnp.bfloat16)

    load(0).wait()

    def send_kv(i, _):
        _, valid, thead = target(i)

        @pl.when(valid)
        def _():
            keys, values = cube_pairs(thead)
            kv_stage[thead, 0:QT] = keys
            kv_stage[thead, QT:] = values
            kv_copy(i).start()
            list_copy(i).start()

        return 0

    lax.fori_loop(1, CHIPS, send_kv, 0)

    @pl.when(has_head)
    def _():
        keys, values = cube_pairs(head)
        kvbuf[pl.ds(me * 2 * QT, QT)] = keys
        kvbuf[pl.ds(me * 2 * QT + QT, QT)] = values
        forward(chip).start()
        lists[pl.ds(pl.multiple_of(chip * QT, QT), QT)] = codes_ref[...]

    load(1).wait()

    def make_q(i, _):
        _, valid, thead = target(i)

        @pl.when(valid)
        def _():
            q_stage[thead] = cube_query(thead)

        return 0

    lax.fori_loop(1, CHIPS, make_q, 0)

    def send_q(n, _):
        i, ch = 1 + n % (CHIPS - 1), n // (CHIPS - 1)
        _, valid, _ = target(i)

        @pl.when(valid)
        def _():
            q_copy(i, ch).start()

        return 0

    lax.fori_loop(0, NCH * (CHIPS - 1), send_q, 0)

    @pl.when(has_head)
    def _():
        qbuf[pl.ds(pl.multiple_of(chip * ROWS, ROWS), ROWS)] = cube_query(head)

    load(2).wait()

    def cube_tokens(n, _):
        cols = pl.ds(pl.multiple_of(n * NCOL, NCOL), NCOL)
        tok_cube[:, cols] = jnp.dot(perm[...], tok[:, cols],
                                    preferred_element_type=jnp.float32).astype(jnp.bfloat16)
        return 0

    lax.fori_loop(0, D // NCOL, cube_tokens, 0)

    @pl.when(has_head)
    def _():
        def pass_on(i, _):
            src = origin(i)
            remote(kv_stage.at[0], block(kvbuf, 2 * src + core, 2 * QT), ksend.at[0],
                   krecv.at[src], sibling).wait_recv()
            forward(src).start()
            return 0

        lax.fori_loop(1, CHIPS, pass_on, 0)

        def small(i, _):
            src = origin(i)
            remote(codes_ref, block(lists, src, QT), lsend.at[0], lrecv.at[src],
                   sibling).wait_recv()
            return 0

        lax.fori_loop(1, CHIPS, small, 0)

        to_smem = pltpu.make_async_copy(lists, lists_smem, smem_sem)
        to_smem.start()

        def passed(src, _):
            part = block(kvbuf, 2 * src + 1 - core, 2 * QT)
            remote(part, part, fsend.at[src], frecv.at[src], sibling).wait_recv()
            return 0

        lax.fori_loop(0, CHIPS, passed, 0)
        to_smem.wait()

    load(3).wait()

    def o_rows(src, j):
        return pl.ds(pl.multiple_of(src * ROWS + j * TILE, TILE), TILE)

    def attend(src, j):
        q = qbuf[o_rows(src, j), :]
        row = src * QT + j
        ks, vs, marks = [], [], []
        for e in range(LIST):
            ks.append(kvbuf[lists_smem[row, e]])
            vs.append(kvbuf[lists_smem[row, 16 + e]])
            marks.append(ones[lists_smem[row, 32 + e]])
        scores = lax.dot_general(q, jnp.concatenate(ks, 0), (((1,), (1,)), ((), ())),
                                 preferred_element_type=jnp.float32)
        top = jnp.max(scores, axis=-1, keepdims=True)
        weights = jnp.exp2((scores - top) * EXP_SCALE).astype(jnp.bfloat16)
        sums = jnp.concatenate([jnp.concatenate(vs, 0), jnp.concatenate(marks, 0)], 1)
        both = jnp.dot(weights, sums, preferred_element_type=jnp.float32)
        obuf[o_rows(src, j), :] = (both[:, :HEAD_DIM] / both[:, HEAD_DIM:]).astype(jnp.bfloat16)

    def send_o(src, j):
        part = obuf.at[o_rows(src, j)]
        place = orecv.at[head, pl.ds(pl.multiple_of(j * TILE, TILE), TILE)]
        sem = orecv_sem.at[j * HEADS + head]

        @pl.when(src != chip)
        def _():
            remote(part, place, osend.at[src], sem, (sec, 2 * src + core)).start()

        @pl.when(src == chip)
        def _():
            pltpu.make_async_copy(part, place, sem).start()

    def y_copy(ch):
        rows = pl.ds(pl.multiple_of(ch * CHUNK, CHUNK), CHUNK)
        return remote(ystage.at[rows], yrecv.at[rows], ysend.at[ch], yrecv_sem.at[ch], ahead)

    def q_wait(src, ch):
        @pl.when(src != chip)
        def _():
            remote(q_stage.at[0, pl.ds(0, CHUNK)], qbuf.at[q_rows(src, ch)], qsend.at[0],
                   qrecv.at[src * NCH + ch], sibling).wait_recv()

    def chunk_step(ch, _):
        @pl.when(has_head & (ch < NCH))
        def _():
            def group(g, _):
                j = ch * JT + g // (CHIPS // UNROLL)
                first = (g % (CHIPS // UNROLL)) * UNROLL
                sources = [origin((first + u + 1) % CHIPS) for u in range(UNROLL)]

                @pl.when(j == ch * JT)
                def _():
                    for src in sources:
                        q_wait(src, ch)

                for src in sources:
                    attend(src, j)
                for src in sources:
                    send_o(src, j)
                return 0

            lax.fori_loop(0, JT * CHIPS // UNROLL, group, 0)

        @pl.when(ch >= 1)
        def _():
            done = ch - 1

            def arrived(k, _):
                j = done * JT + k // HEADS
                h = k % HEADS
                place = orecv.at[h, pl.ds(pl.multiple_of(j * TILE, TILE), TILE)]
                pltpu.make_async_copy(obuf.at[pl.ds(0, TILE)], place,
                                      orecv_sem.at[j * HEADS + h]).wait()
                return 0

            lax.fori_loop(0, JT * HEADS, arrived, 0)
            rows = pl.ds(pl.multiple_of(done * CHUNK, CHUNK), CHUNK)
            attended = jnp.concatenate([orecv[h, rows, :] for h in range(HEADS)], axis=1)

            def project(n, _):
                cols = pl.ds(pl.multiple_of(n * NCOL, NCOL), NCOL)
                acc = jnp.dot(attended, w[:, cols], preferred_element_type=jnp.float32)
                ystage[rows, cols] = (
                    tok_cube[rows, cols].astype(jnp.float32) + gate_ref[0:1, cols] * acc
                ).astype(jnp.bfloat16)
                return 0

            lax.fori_loop(0, D // NCOL, project, 0)
            y_copy(done).start()

        return 0

    lax.fori_loop(0, NCH + 1, chunk_step, 0)

    order_copy().wait()

    def y_wait(ch, _):
        y_copy(ch).wait()
        return 0

    lax.fori_loop(0, NCH, y_wait, 0)

    def drain(i, _):
        _, valid, thead = target(i)

        @pl.when(valid)
        def _():
            kv_copy(i).wait_send()
            remote(q_stage.at[thead], block(qbuf, chip, ROWS), qsend.at[thead], qrecv.at[0],
                   sibling).wait_send()
            list_copy(i).wait_send()

        return 0

    lax.fori_loop(1, CHIPS, drain, 0)

    @pl.when(has_head)
    def _():
        def drain_head(src, _):
            forward(src).wait_send()

            @pl.when(src != chip)
            def _():
                part = block(obuf, src, ROWS)
                remote(part, part, osend.at[src], orecv_sem.at[0], sibling).wait_send()

            return 0

        lax.fori_loop(0, CHIPS, drain_head, 0)


def restore(order_ref, rows_ref, out_ref):
    perm = (
        lax.broadcasted_iota(jnp.int32, (ROWS, ROWS), 0) == order_ref[...]
    ).astype(jnp.bfloat16)
    out_ref[...] = jnp.dot(perm, rows_ref[...],
                           preferred_element_type=jnp.float32).astype(jnp.bfloat16)


def body(tokens, queries, keyvals, out_weight, gate, cube_order, crit_owner, crit_tile, crit_count):
    live = jnp.arange(LIST, dtype=jnp.int32)[None, :] < crit_count[0][:, None]
    k_at = crit_owner[0] * (2 * QT) + crit_tile[0]
    v_at = jnp.where(live, k_at + QT, KV_TILES)
    m_at = jnp.where(live, 0, 1)

    def wide(part):
        return jnp.pad(part, ((0, 0), (0, 16 - LIST)))

    codes = jnp.concatenate([wide(k_at), wide(v_at), wide(m_at)], axis=1)
    codes = jnp.pad(codes, ((0, 0), (0, 128 - codes.shape[1])))
    bf16, i32 = jnp.bfloat16, jnp.int32
    dma = pltpu.SemaphoreType.DMA
    rows, order = pl.pallas_call(
        kernel,
        out_shape=(
            jax.ShapeDtypeStruct((ROWS, D), bf16),
            jax.ShapeDtypeStruct((1, ROWS), i32),
        ),
        in_specs=[pl.BlockSpec(memory_space=pl.ANY)] * 4
        + [pl.BlockSpec(memory_space=pltpu.VMEM)] * 3,
        out_specs=(
            pl.BlockSpec(memory_space=pl.ANY),
            pl.BlockSpec(memory_space=pl.ANY),
        ),
        scratch_shapes=[
            pltpu.VMEM((ROWS, D), bf16),
            pltpu.VMEM((ROWS, HW), bf16),
            pltpu.VMEM((ROWS, 2, HW), bf16),
            pltpu.VMEM((HW, D), bf16),
            pltpu.VMEM((ROWS, ROWS), bf16),
            pltpu.VMEM((ROWS, D), bf16),
            pltpu.VMEM((HEADS, 2 * QT, TILE, HEAD_DIM), bf16),
            pltpu.VMEM((HEADS, ROWS, HEAD_DIM), bf16),
            pltpu.VMEM((KV_TILES + 1, TILE, HEAD_DIM), bf16),
            pltpu.VMEM((CHIPS * ROWS, HEAD_DIM), bf16),
            pltpu.VMEM((CHIPS * ROWS, HEAD_DIM), bf16),
            pltpu.VMEM((2, TILE, HEAD_DIM), bf16),
            pltpu.VMEM((CHIPS * QT, 128), i32),
            pltpu.SMEM((CHIPS * QT, 128), i32),
            pltpu.VMEM((HEADS, ROWS, HEAD_DIM), bf16),
            pltpu.VMEM((ROWS, D), bf16),
            dma((4,)), dma, dma((HEADS,)), dma((CHIPS,)), dma((CHIPS,)), dma((CHIPS,)),
            dma((HEADS,)), dma((CHIPS * NCH,)), dma((HEADS,)), dma((CHIPS,)),
            dma((CHIPS,)), dma((QT * HEADS,)), dma((NCH,)), dma((NCH,)), dma, dma,
        ],
        compiler_params=pltpu.CompilerParams(
            collective_id=0, has_side_effects=True, vmem_limit_bytes=60 * 2**20
        ),
        cost_estimate=pl.CostEstimate(
            flops=16 * 10**9, bytes_accessed=22 * 2**20, transcendentals=10**7
        ),
        name="cube_attention",
    )(tokens[0], queries[0], keyvals[0], out_weight[0], gate, cube_order[0], codes)
    handed = pl.pallas_call(
        restore,
        out_shape=jax.ShapeDtypeStruct((ROWS, D), bf16),
        grid=(D // NCOL,),
        in_specs=[
            pl.BlockSpec((1, ROWS), lambda n: (0, 0)),
            pl.BlockSpec((ROWS, NCOL), lambda n: (0, n)),
        ],
        out_specs=pl.BlockSpec((ROWS, NCOL), lambda n: (0, n)),
        name="token_order",
    )(order, rows)
    return handed[None]


def solution(mesh):
    in_specs = (
        P("section", "ctx", None),
        P("section", "ctx", None),
        P("section", "ctx", None, None),
        P("section", None, None),
        P("section", None),
        P("section", "ctx", None),
        P("section", "ctx", None),
        P("section", "ctx", None),
        P("section", "ctx"),
    )
    out_specs = P("section", "ctx", None)
    return jax.shard_map(body, mesh=mesh, in_specs=in_specs, out_specs=out_specs, check_vma=False)
```

```python
import math

import jax
import jax.numpy as jnp
from jax import lax
from jax.experimental import pallas as pl
from jax.experimental.pallas import tpu as pltpu
from jax.sharding import PartitionSpec as P

D = 3072
HEADS = 12
HEAD_DIM = 128
TILE = 64
LIST = 12
QT = 8
HW = 1536
ROWS = 512
CTX = 32
SIDE = 4
CHIPS = 16
SECTIONS = 4
KV_TILES = CTX * 2 * QT
JT = 1
CHUNK = JT * TILE
NCH = QT // JT
UNROLL = 8
Q_FIRST = 1
LAG = 1
HOP = 2
Y_COLS = 2560
NCOL = 512
EXP_SCALE = math.log2(math.e) / math.sqrt(HEAD_DIM)


def kernel(
    tok_hbm, q_hbm, kv_hbm, w_hbm, gate_ref, order_ref, codes_ref, yrecv, prev_order,
    tok, q_in, kv_in, w, perm, tok_cube, kv_stage, q_stage, kvbuf, qbuf, obuf, ones,
    lists, lists_smem, orecv, ystage, relay,
    load_sem, smem_sem, ksend, krecv, fsend, frecv, qsend, qrecv, lsend, lrecv,
    osend, orecv_sem, ysend, yrecv_sem, bsend, brecv, psend, precv,
):
    sec = lax.axis_index("section")
    me = lax.axis_index("ctx")
    core = me % 2
    chip = me // 2
    cx, cz = chip // SIDE, chip % SIDE
    kind = (cz - cx + 3) % SIDE
    has_head = kind < 3
    head = cx + SIDE * kind
    sibling = (sec, me + 1 - 2 * core)
    ahead = ((sec + 1) % SECTIONS, me)
    behind = ((sec + SECTIONS - 1) % SECTIONS, me)

    def remote(src, dst, send, recv, device):
        return pltpu.make_async_remote_copy(
            src_ref=src, dst_ref=dst, send_sem=send, recv_sem=recv,
            device_id=device, device_id_type=pl.DeviceIdType.MESH,
        )

    def load(i):
        src = (kv_hbm, q_hbm, tok_hbm, w_hbm)[i]
        return pltpu.make_async_copy(src, (kv_in, q_in, tok, w)[i], load_sem.at[i])

    load(0).start()

    barrier = pltpu.get_barrier_semaphore()

    def greet(i, _):
        other = (chip + i) % CHIPS
        pl.semaphore_signal(barrier, inc=1, device_id=(sec, 2 * other + core),
                            device_id_type=pl.DeviceIdType.MESH)
        return 0

    lax.fori_loop(1, CHIPS, greet, 0)
    for device in (sibling, ahead, behind):
        pl.semaphore_signal(barrier, inc=1, device_id=device,
                            device_id_type=pl.DeviceIdType.MESH)

    column = jnp.transpose(jnp.broadcast_to(order_ref[...], (128, ROWS)))[:, :1]
    perm[...] = (lax.broadcasted_iota(jnp.int32, (ROWS, ROWS), 1) == column).astype(jnp.bfloat16)
    ones[0] = jnp.ones((TILE, HEAD_DIM), jnp.bfloat16)
    ones[1] = jnp.zeros((TILE, HEAD_DIM), jnp.bfloat16)
    kvbuf[KV_TILES] = jnp.zeros((TILE, HEAD_DIM), jnp.bfloat16)

    pl.semaphore_wait(barrier, CHIPS + 2)

    def order_copy():
        return remote(order_ref, prev_order, psend, precv, ahead)

    order_copy().start()

    def shift(i):
        return i % SIDE, (i // SIDE + 3 * (i % SIDE)) % SIDE

    def target(i):
        dx, dz = shift(i)
        tx, tz = (cx + dx) % SIDE, (cz + dz) % SIDE
        tkind = (tz - tx + 3) % SIDE
        return tx * SIDE + tz, tkind < 3, tx + SIDE * tkind

    def origin(i):
        dx, dz = shift(i)
        return ((cx + SIDE - dx) % SIDE) * SIDE + (cz + SIDE - dz) % SIDE

    def block(ref, index, rows):
        return ref.at[pl.ds(pl.multiple_of(index * rows, rows), rows)]

    def list_copy(i):
        to, _, thead = target(i)
        return remote(codes_ref, block(lists, chip, QT), lsend.at[thead], lrecv.at[chip],
                      (sec, 2 * to + core))

    def kv_copy(i):
        to, _, thead = target(i)
        return remote(kv_stage.at[thead], block(kvbuf, me, 2 * QT), ksend.at[thead],
                      krecv.at[chip], (sec, 2 * to + core))

    def q_rows(src, ch):
        return pl.ds(pl.multiple_of(src * ROWS + ch * CHUNK, CHUNK), CHUNK)

    def q_copy(i, ch):
        to, _, thead = target(i)
        rows = pl.ds(pl.multiple_of(ch * CHUNK, CHUNK), CHUNK)
        return remote(q_stage.at[thead, rows], qbuf.at[q_rows(chip, ch)], qsend.at[thead],
                      qrecv.at[chip * NCH + ch], (sec, 2 * to + core))

    def forward(from_chip):
        part = block(kvbuf, 2 * from_chip + core, 2 * QT)
        return remote(part, part, fsend.at[from_chip], frecv.at[from_chip], sibling)

    def lanes(h):
        return pl.ds(pl.multiple_of(h * HEAD_DIM, HEAD_DIM), HEAD_DIM)

    def cube_pairs(h):
        both = jnp.concatenate([kv_in[:, 0, lanes(h)], kv_in[:, 1, lanes(h)]], axis=1)
        rows = jnp.dot(perm[...], both, preferred_element_type=jnp.float32).astype(jnp.bfloat16)
        rows = rows.reshape(QT, TILE, 2 * HEAD_DIM)
        return rows[:, :, :HEAD_DIM], rows[:, :, HEAD_DIM:]

    def cube_query(h):
        return jnp.dot(perm[...], q_in[:, lanes(h)],
                       preferred_element_type=jnp.float32).astype(jnp.bfloat16)

    load(0).wait()
    for i in range(1, 4):
        load(i).start()

    def send_kv(i, _):
        _, valid, thead = target(i)

        @pl.when(valid)
        def _():
            keys, values = cube_pairs(thead)
            kv_stage[thead, 0:QT] = keys
            kv_stage[thead, QT:] = values
            kv_copy(i).start()
            list_copy(i).start()

        return 0

    lax.fori_loop(1, CHIPS, send_kv, 0)

    @pl.when(has_head)
    def _():
        keys, values = cube_pairs(head)
        kvbuf[pl.ds(me * 2 * QT, QT)] = keys
        kvbuf[pl.ds(me * 2 * QT + QT, QT)] = values
        forward(chip).start()
        lists[pl.ds(pl.multiple_of(chip * QT, QT), QT)] = codes_ref[...]

    load(1).wait()

    def make_q(i, _):
        _, valid, thead = target(i)

        @pl.when(valid)
        def _():
            q_stage[thead] = cube_query(thead)

        return 0

    lax.fori_loop(1, CHIPS, make_q, 0)

    def send_q(ch):
        def one(i, _):
            _, valid, _ = target(i)

            @pl.when(valid)
            def _():
                q_copy(i, ch).start()

            return 0

        lax.fori_loop(1, CHIPS, one, 0)

    for ch in range(Q_FIRST):
        send_q(ch)

    @pl.when(has_head)
    def _():
        qbuf[pl.ds(pl.multiple_of(chip * ROWS, ROWS), ROWS)] = cube_query(head)

    load(2).wait()

    def cube_tokens(n, _):
        cols = pl.ds(pl.multiple_of(n * NCOL, NCOL), NCOL)
        tok_cube[:, cols] = jnp.dot(perm[...], tok[:, cols],
                                    preferred_element_type=jnp.float32).astype(jnp.bfloat16)
        return 0

    lax.fori_loop(0, D // NCOL, cube_tokens, 0)

    @pl.when(has_head)
    def _():
        def pass_on(i, _):
            src = origin(i)
            remote(kv_stage.at[0], block(kvbuf, 2 * src + core, 2 * QT), ksend.at[0],
                   krecv.at[src], sibling).wait_recv()
            forward(src).start()
            return 0

        lax.fori_loop(1, CHIPS, pass_on, 0)

        def small(i, _):
            src = origin(i)
            remote(codes_ref, block(lists, src, QT), lsend.at[0], lrecv.at[src],
                   sibling).wait_recv()
            return 0

        lax.fori_loop(1, CHIPS, small, 0)

        to_smem = pltpu.make_async_copy(lists, lists_smem, smem_sem)
        to_smem.start()

        def passed(src, _):
            part = block(kvbuf, 2 * src + 1 - core, 2 * QT)
            remote(part, part, fsend.at[src], frecv.at[src], sibling).wait_recv()
            return 0

        lax.fori_loop(0, CHIPS, passed, 0)
        to_smem.wait()

    load(3).wait()

    def o_rows(src, j):
        return pl.ds(pl.multiple_of(src * ROWS + j * TILE, TILE), TILE)

    def attend(src, j):
        q = qbuf[o_rows(src, j), :]
        row = src * QT + j
        ks, vs, marks = [], [], []
        for e in range(LIST):
            ks.append(kvbuf[lists_smem[row, e]])
            vs.append(kvbuf[lists_smem[row, 16 + e]])
            marks.append(ones[lists_smem[row, 32 + e]])
        scores = lax.dot_general(q, jnp.concatenate(ks, 0), (((1,), (1,)), ((), ())),
                                 preferred_element_type=jnp.float32)
        top = jnp.max(scores, axis=-1, keepdims=True)
        weights = jnp.exp2((scores - top) * EXP_SCALE).astype(jnp.bfloat16)
        sums = jnp.concatenate([jnp.concatenate(vs, 0), jnp.concatenate(marks, 0)], 1)
        both = jnp.dot(weights, sums, preferred_element_type=jnp.float32)
        obuf[o_rows(src, j), :] = (both[:, :HEAD_DIM] / both[:, HEAD_DIM:]).astype(jnp.bfloat16)

    def send_o(src, j):
        part = obuf.at[o_rows(src, j)]
        place = orecv.at[head, pl.ds(pl.multiple_of(j * TILE, TILE), TILE)]
        sem = orecv_sem.at[j * HEADS + head]

        @pl.when(src != chip)
        def _():
            remote(part, place, osend.at[src], sem, (sec, 2 * src + core)).start()

        @pl.when(src == chip)
        def _():
            pltpu.make_async_copy(part, place, sem).start()

    def y_copy(ch):
        rows = pl.ds(pl.multiple_of(ch * CHUNK, CHUNK), CHUNK)
        cols = pl.ds(0, Y_COLS)
        return remote(ystage.at[rows, cols], yrecv.at[rows, cols], ysend.at[ch],
                      yrecv_sem.at[ch], ahead)

    def back_copy(hop, ch):
        rows = pl.ds(pl.multiple_of(ch * CHUNK, CHUNK), CHUNK)
        cols = pl.ds(Y_COLS, D - Y_COLS)
        if hop == 0:
            src, dst = ystage.at[rows, cols], relay.at[0, rows]
        elif hop == 1:
            src, dst = relay.at[0, rows], relay.at[1, rows]
        else:
            src, dst = relay.at[1, rows], yrecv.at[rows, cols]
        return remote(src, dst, bsend.at[hop, ch], brecv.at[hop, ch], behind)

    def q_wait(src, ch):
        @pl.when(src != chip)
        def _():
            remote(q_stage.at[0, pl.ds(0, CHUNK)], qbuf.at[q_rows(src, ch)], qsend.at[0],
                   qrecv.at[src * NCH + ch], sibling).wait_recv()

    def chunk_step(ch, _):
        @pl.when(ch + Q_FIRST < NCH)
        def _():
            send_q(ch + Q_FIRST)

        for hop in (2, 1):
            moved = ch - LAG - HOP * hop

            @pl.when((moved >= 0) & (moved < NCH))
            def _():
                back_copy(hop - 1, moved).wait_recv()
                back_copy(hop, moved).start()

        @pl.when(has_head & (ch < NCH))
        def _():
            def group(g, _):
                j = ch * JT + g // (CHIPS // UNROLL)
                first = (g % (CHIPS // UNROLL)) * UNROLL
                sources = [origin((first + u + 1) % CHIPS) for u in range(UNROLL)]

                @pl.when(j == ch * JT)
                def _():
                    for src in sources:
                        q_wait(src, ch)

                for src in sources:
                    attend(src, j)
                for src in sources:
                    send_o(src, j)
                return 0

            lax.fori_loop(0, JT * CHIPS // UNROLL, group, 0)

        @pl.when((ch >= LAG) & (ch < NCH + LAG))
        def _():
            done = ch - LAG

            def arrived(k, _):
                j = done * JT + k // HEADS
                h = k % HEADS
                place = orecv.at[h, pl.ds(pl.multiple_of(j * TILE, TILE), TILE)]
                pltpu.make_async_copy(obuf.at[pl.ds(0, TILE)], place,
                                      orecv_sem.at[j * HEADS + h]).wait()
                return 0

            lax.fori_loop(0, JT * HEADS, arrived, 0)
            rows = pl.ds(pl.multiple_of(done * CHUNK, CHUNK), CHUNK)
            attended = jnp.concatenate([orecv[h, rows, :] for h in range(HEADS)], axis=1)

            def project(n, _):
                cols = pl.ds(pl.multiple_of(n * NCOL, NCOL), NCOL)
                acc = jnp.dot(attended, w[:, cols], preferred_element_type=jnp.float32)
                ystage[rows, cols] = (
                    tok_cube[rows, cols].astype(jnp.float32) + gate_ref[0:1, cols] * acc
                ).astype(jnp.bfloat16)
                return 0

            lax.fori_loop(0, D // NCOL, project, 0)
            back_copy(0, done).start()
            y_copy(done).start()

        return 0

    lax.fori_loop(0, NCH + LAG + 2 * HOP, chunk_step, 0)

    order_copy().wait()

    def y_wait(ch, _):
        y_copy(ch).wait()
        for hop in range(3):
            back_copy(hop, ch).wait_send()
        back_copy(2, ch).wait_recv()
        return 0

    lax.fori_loop(0, NCH, y_wait, 0)

    def drain(i, _):
        _, valid, thead = target(i)

        @pl.when(valid)
        def _():
            kv_copy(i).wait_send()
            remote(q_stage.at[thead], block(qbuf, chip, ROWS), qsend.at[thead], qrecv.at[0],
                   sibling).wait_send()
            list_copy(i).wait_send()

        return 0

    lax.fori_loop(1, CHIPS, drain, 0)

    @pl.when(has_head)
    def _():
        def drain_head(src, _):
            forward(src).wait_send()

            @pl.when(src != chip)
            def _():
                part = block(obuf, src, ROWS)
                remote(part, part, osend.at[src], orecv_sem.at[0], sibling).wait_send()

            return 0

        lax.fori_loop(0, CHIPS, drain_head, 0)


def restore(order_ref, rows_ref, out_ref, perm):
    @pl.when(pl.program_id(0) == 0)
    def _():
        perm[...] = (
            lax.broadcasted_iota(jnp.int32, (ROWS, ROWS), 0) == order_ref[...]
        ).astype(jnp.bfloat16)

    out_ref[...] = jnp.dot(perm[...], rows_ref[...],
                           preferred_element_type=jnp.float32).astype(jnp.bfloat16)


def body(tokens, queries, keyvals, out_weight, gate, cube_order, crit_owner, crit_tile, crit_count):
    live = jnp.arange(LIST, dtype=jnp.int32)[None, :] < crit_count[0][:, None]
    k_at = crit_owner[0] * (2 * QT) + crit_tile[0]
    v_at = jnp.where(live, k_at + QT, KV_TILES)
    m_at = jnp.where(live, 0, 1)

    def wide(part):
        return jnp.pad(part, ((0, 0), (0, 16 - LIST)))

    codes = jnp.concatenate([wide(k_at), wide(v_at), wide(m_at)], axis=1)
    codes = jnp.pad(codes, ((0, 0), (0, 128 - codes.shape[1])))
    bf16, i32 = jnp.bfloat16, jnp.int32
    dma = pltpu.SemaphoreType.DMA
    rows, order = pl.pallas_call(
        kernel,
        out_shape=(
            jax.ShapeDtypeStruct((ROWS, D), bf16),
            jax.ShapeDtypeStruct((1, ROWS), i32),
        ),
        in_specs=[pl.BlockSpec(memory_space=pl.ANY)] * 4
        + [pl.BlockSpec(memory_space=pltpu.VMEM)] * 3,
        out_specs=(
            pl.BlockSpec(memory_space=pl.ANY),
            pl.BlockSpec(memory_space=pl.ANY),
        ),
        scratch_shapes=[
            pltpu.VMEM((ROWS, D), bf16),
            pltpu.VMEM((ROWS, HW), bf16),
            pltpu.VMEM((ROWS, 2, HW), bf16),
            pltpu.VMEM((HW, D), bf16),
            pltpu.VMEM((ROWS, ROWS), bf16),
            pltpu.VMEM((ROWS, D), bf16),
            pltpu.VMEM((HEADS, 2 * QT, TILE, HEAD_DIM), bf16),
            pltpu.VMEM((HEADS, ROWS, HEAD_DIM), bf16),
            pltpu.VMEM((KV_TILES + 1, TILE, HEAD_DIM), bf16),
            pltpu.VMEM((CHIPS * ROWS, HEAD_DIM), bf16),
            pltpu.VMEM((CHIPS * ROWS, HEAD_DIM), bf16),
            pltpu.VMEM((2, TILE, HEAD_DIM), bf16),
            pltpu.VMEM((CHIPS * QT, 128), i32),
            pltpu.SMEM((CHIPS * QT, 128), i32),
            pltpu.VMEM((HEADS, ROWS, HEAD_DIM), bf16),
            pltpu.VMEM((ROWS, D), bf16),
            pltpu.VMEM((2, ROWS, D - Y_COLS), bf16),
            dma((4,)), dma, dma((HEADS,)), dma((CHIPS,)), dma((CHIPS,)), dma((CHIPS,)),
            dma((HEADS,)), dma((CHIPS * NCH,)), dma((HEADS,)), dma((CHIPS,)),
            dma((CHIPS,)), dma((QT * HEADS,)), dma((NCH,)), dma((NCH,)), dma((3, NCH)), dma((3, NCH)),
            dma, dma,
        ],
        compiler_params=pltpu.CompilerParams(
            collective_id=0, has_side_effects=True, vmem_limit_bytes=60 * 2**20
        ),
        cost_estimate=pl.CostEstimate(
            flops=16 * 10**9, bytes_accessed=22 * 2**20, transcendentals=10**7
        ),
        name="cube_attention",
    )(tokens[0], queries[0], keyvals[0], out_weight[0], gate, cube_order[0], codes)
    handed = pl.pallas_call(
        restore,
        out_shape=jax.ShapeDtypeStruct((ROWS, D), bf16),
        grid=(D // NCOL,),
        in_specs=[
            pl.BlockSpec((1, ROWS), lambda n: (0, 0)),
            pl.BlockSpec((ROWS, NCOL), lambda n: (0, n)),
        ],
        out_specs=pl.BlockSpec((ROWS, NCOL), lambda n: (0, n)),
        scratch_shapes=[pltpu.VMEM((ROWS, ROWS), bf16)],
        name="token_order",
    )(order, rows)
    return handed[None]


def solution(mesh):
    in_specs = (
        P("section", "ctx", None),
        P("section", "ctx", None),
        P("section", "ctx", None, None),
        P("section", None, None),
        P("section", None),
        P("section", "ctx", None),
        P("section", "ctx", None),
        P("section", "ctx", None),
        P("section", "ctx"),
    )
    out_specs = P("section", "ctx", None)
    return jax.shard_map(body, mesh=mesh, in_specs=in_specs, out_specs=out_specs, check_vma=False)
```

```python
import math

import jax
import jax.numpy as jnp
from jax import lax
from jax.experimental import pallas as pl
from jax.experimental.pallas import tpu as pltpu
from jax.sharding import PartitionSpec as P

D = 3072
HEADS = 12
HEAD_DIM = 128
TILE = 64
LIST = 12
QT = 8
HW = 1536
ROWS = 512
CTX = 32
SIDE = 4
CHIPS = 16
SECTIONS = 4
KV_TILES = CTX * 2 * QT
JT = 1
CHUNK = JT * TILE
NCH = QT // JT
UNROLL = 8
Q_FIRST = 1
LAG = 1
HOP = 2
Y_COLS = 2304
ROUND = 7
NCOL = 512
R_COLS = 1024
EXP_SCALE = math.log2(math.e) / math.sqrt(HEAD_DIM)


def kernel(
    tok_hbm, q_hbm, kv_hbm, w_hbm, gate_ref, order_ref, codes_ref, yrecv, prev_order,
    tok, q_in, kv_in, w, perm, tok_cube, kv_stage, q_stage, kvbuf, qbuf, obuf, ones,
    lists, lists_smem, orecv, ystage, relay,
    load_sem, smem_sem, ksend, krecv, fsend, frecv, qsend, qrecv, lsend, lrecv,
    osend, orecv_sem, ysend, yrecv_sem, bsend, brecv, psend, precv,
):
    sec = lax.axis_index("section")
    me = lax.axis_index("ctx")
    core = me % 2
    chip = me // 2
    cx, cz = chip // SIDE, chip % SIDE
    kind = (cz - cx + 3) % SIDE
    has_head = kind < 3
    head = cx + SIDE * kind
    sibling = (sec, me + 1 - 2 * core)
    ahead = ((sec + 1) % SECTIONS, me)
    behind = ((sec + SECTIONS - 1) % SECTIONS, me)

    def remote(src, dst, send, recv, device):
        return pltpu.make_async_remote_copy(
            src_ref=src, dst_ref=dst, send_sem=send, recv_sem=recv,
            device_id=device, device_id_type=pl.DeviceIdType.MESH,
        )

    def load(i):
        src = (kv_hbm, q_hbm, tok_hbm, w_hbm)[i]
        return pltpu.make_async_copy(src, (kv_in, q_in, tok, w)[i], load_sem.at[i])

    load(0).start()

    barrier = pltpu.get_barrier_semaphore()

    def greet(i, _):
        other = (chip + i) % CHIPS
        pl.semaphore_signal(barrier, inc=1, device_id=(sec, 2 * other + core),
                            device_id_type=pl.DeviceIdType.MESH)
        return 0

    lax.fori_loop(1, CHIPS, greet, 0)
    for device in (sibling, ahead, behind):
        pl.semaphore_signal(barrier, inc=1, device_id=device,
                            device_id_type=pl.DeviceIdType.MESH)

    column = jnp.transpose(jnp.broadcast_to(order_ref[...], (128, ROWS)))[:, :1]
    perm[...] = (lax.broadcasted_iota(jnp.int32, (ROWS, ROWS), 1) == column).astype(jnp.bfloat16)
    ones[0] = jnp.ones((TILE, HEAD_DIM), jnp.bfloat16)
    ones[1] = jnp.zeros((TILE, HEAD_DIM), jnp.bfloat16)
    kvbuf[KV_TILES] = jnp.zeros((TILE, HEAD_DIM), jnp.bfloat16)

    pl.semaphore_wait(barrier, CHIPS + 2)

    def order_copy():
        return remote(order_ref, prev_order, psend, precv, ahead)

    order_copy().start()

    def shift(i):
        return i % SIDE, (i // SIDE + 3 * (i % SIDE)) % SIDE

    def target(i):
        dx, dz = shift(i)
        tx, tz = (cx + dx) % SIDE, (cz + dz) % SIDE
        tkind = (tz - tx + 3) % SIDE
        return tx * SIDE + tz, tkind < 3, tx + SIDE * tkind

    def origin(i):
        dx, dz = shift(i)
        return ((cx + SIDE - dx) % SIDE) * SIDE + (cz + SIDE - dz) % SIDE

    def block(ref, index, rows):
        return ref.at[pl.ds(pl.multiple_of(index * rows, rows), rows)]

    def list_copy(i):
        to, _, thead = target(i)
        return remote(codes_ref, block(lists, chip, QT), lsend.at[thead], lrecv.at[chip],
                      (sec, 2 * to + core))

    def kv_copy(i):
        to, _, thead = target(i)
        return remote(kv_stage.at[thead], block(kvbuf, me, 2 * QT), ksend.at[thead],
                      krecv.at[chip], (sec, 2 * to + core))

    def q_rows(src, ch):
        return pl.ds(pl.multiple_of(src * ROWS + ch * CHUNK, CHUNK), CHUNK)

    def q_copy(i, ch):
        to, _, thead = target(i)
        rows = pl.ds(pl.multiple_of(ch * CHUNK, CHUNK), CHUNK)
        return remote(q_stage.at[thead, rows], qbuf.at[q_rows(chip, ch)], qsend.at[thead],
                      qrecv.at[chip * NCH + ch], (sec, 2 * to + core))

    def forward(from_chip):
        part = block(kvbuf, 2 * from_chip + core, 2 * QT)
        return remote(part, part, fsend.at[from_chip], frecv.at[from_chip], sibling)

    def lanes(h):
        return pl.ds(pl.multiple_of(h * HEAD_DIM, HEAD_DIM), HEAD_DIM)

    def cube_pairs(h):
        both = jnp.concatenate([kv_in[:, 0, lanes(h)], kv_in[:, 1, lanes(h)]], axis=1)
        rows = jnp.dot(perm[...], both, preferred_element_type=jnp.float32).astype(jnp.bfloat16)
        rows = rows.reshape(QT, TILE, 2 * HEAD_DIM)
        return rows[:, :, :HEAD_DIM], rows[:, :, HEAD_DIM:]

    def cube_query(h):
        return jnp.dot(perm[...], q_in[:, lanes(h)],
                       preferred_element_type=jnp.float32).astype(jnp.bfloat16)

    load(0).wait()
    for i in range(1, 4):
        load(i).start()

    def send_kv(i, _):
        _, valid, thead = target(i)

        @pl.when(valid)
        def _():
            keys, values = cube_pairs(thead)
            kv_stage[thead, 0:QT] = keys
            kv_stage[thead, QT:] = values
            kv_copy(i).start()
            list_copy(i).start()

        return 0

    lax.fori_loop(1, CHIPS, send_kv, 0)

    @pl.when(has_head)
    def _():
        keys, values = cube_pairs(head)
        kvbuf[pl.ds(me * 2 * QT, QT)] = keys
        kvbuf[pl.ds(me * 2 * QT + QT, QT)] = values
        forward(chip).start()
        lists[pl.ds(pl.multiple_of(chip * QT, QT), QT)] = codes_ref[...]

    load(1).wait()

    def make_q(i, _):
        _, valid, thead = target(i)

        @pl.when(valid)
        def _():
            q_stage[thead] = cube_query(thead)

        return 0

    lax.fori_loop(1, CHIPS, make_q, 0)

    def send_q(ch):
        def one(i, _):
            _, valid, _ = target(i)

            @pl.when(valid)
            def _():
                q_copy(i, ch).start()

            return 0

        lax.fori_loop(1, CHIPS, one, 0)

    for ch in range(Q_FIRST):
        send_q(ch)

    @pl.when(has_head)
    def _():
        qbuf[pl.ds(pl.multiple_of(chip * ROWS, ROWS), ROWS)] = cube_query(head)

    load(2).wait()

    def cube_tokens(n, _):
        cols = pl.ds(pl.multiple_of(n * NCOL, NCOL), NCOL)
        tok_cube[:, cols] = jnp.dot(perm[...], tok[:, cols],
                                    preferred_element_type=jnp.float32).astype(jnp.bfloat16)
        return 0

    lax.fori_loop(0, D // NCOL, cube_tokens, 0)

    @pl.when(has_head)
    def _():
        def pass_on(i, _):
            src = origin(i)
            remote(kv_stage.at[0], block(kvbuf, 2 * src + core, 2 * QT), ksend.at[0],
                   krecv.at[src], sibling).wait_recv()
            forward(src).start()
            return 0

        lax.fori_loop(1, CHIPS, pass_on, 0)

        def small(i, _):
            src = origin(i)
            remote(codes_ref, block(lists, src, QT), lsend.at[0], lrecv.at[src],
                   sibling).wait_recv()
            return 0

        lax.fori_loop(1, CHIPS, small, 0)

        to_smem = pltpu.make_async_copy(lists, lists_smem, smem_sem)
        to_smem.start()

        def passed(src, _):
            part = block(kvbuf, 2 * src + 1 - core, 2 * QT)
            remote(part, part, fsend.at[src], frecv.at[src], sibling).wait_recv()
            return 0

        lax.fori_loop(0, CHIPS, passed, 0)
        to_smem.wait()

    load(3).wait()

    def o_rows(src, j):
        return pl.ds(pl.multiple_of(src * ROWS + j * TILE, TILE), TILE)

    def attend(src, j):
        q = qbuf[o_rows(src, j), :]
        row = src * QT + j
        ks, vs, marks = [], [], []
        for e in range(LIST):
            ks.append(kvbuf[lists_smem[row, e]])
            vs.append(kvbuf[lists_smem[row, 16 + e]])
            marks.append(ones[lists_smem[row, 32 + e]])
        scores = lax.dot_general(q, jnp.concatenate(ks, 0), (((1,), (1,)), ((), ())),
                                 preferred_element_type=jnp.float32)
        top = jnp.max(scores, axis=-1, keepdims=True)
        weights = jnp.exp2((scores - top) * EXP_SCALE).astype(jnp.bfloat16)
        sums = jnp.concatenate([jnp.concatenate(vs, 0), jnp.concatenate(marks, 0)], 1)
        both = jnp.dot(weights, sums, preferred_element_type=jnp.float32)
        obuf[o_rows(src, j), :] = (both[:, :HEAD_DIM] / both[:, HEAD_DIM:]).astype(jnp.bfloat16)

    def send_o(src, j):
        part = obuf.at[o_rows(src, j)]
        place = orecv.at[head, pl.ds(pl.multiple_of(j * TILE, TILE), TILE)]
        sem = orecv_sem.at[j * HEADS + head]

        @pl.when(src != chip)
        def _():
            remote(part, place, osend.at[src], sem, (sec, 2 * src + core)).start()

        @pl.when(src == chip)
        def _():
            pltpu.make_async_copy(part, place, sem).start()

    def y_copy(ch):
        rows = pl.ds(pl.multiple_of(ch * CHUNK, CHUNK), CHUNK)
        cols = pl.ds(0, Y_COLS)
        return remote(ystage.at[rows, cols], yrecv.at[rows, cols], ysend.at[ch],
                      yrecv_sem.at[ch], ahead)

    def rest_copy(ch):
        rows = pl.ds(pl.multiple_of(ch * CHUNK, CHUNK), CHUNK)
        cols = pl.ds(Y_COLS, D - Y_COLS)
        return remote(ystage.at[rows, cols], yrecv.at[rows, cols], bsend.at[0, ch],
                      brecv.at[2, ch], ahead)

    def back_copy(hop, ch):
        rows = pl.ds(pl.multiple_of(ch * CHUNK, CHUNK), CHUNK)
        cols = pl.ds(Y_COLS, D - Y_COLS)
        if hop == 0:
            src, dst = ystage.at[rows, cols], relay.at[0, rows]
        elif hop == 1:
            src, dst = relay.at[0, rows], relay.at[1, rows]
        else:
            src, dst = relay.at[1, rows], yrecv.at[rows, cols]
        return remote(src, dst, bsend.at[hop, ch], brecv.at[hop, ch], behind)

    def q_wait(src, ch):
        @pl.when(src != chip)
        def _():
            remote(q_stage.at[0, pl.ds(0, CHUNK)], qbuf.at[q_rows(src, ch)], qsend.at[0],
                   qrecv.at[src * NCH + ch], sibling).wait_recv()

    def chunk_step(ch, _):
        @pl.when(ch + Q_FIRST < NCH)
        def _():
            send_q(ch + Q_FIRST)

        for hop in (2, 1):
            moved = ch - LAG - HOP * hop

            @pl.when((moved >= 0) & (moved < ROUND))
            def _():
                back_copy(hop - 1, moved).wait_recv()
                back_copy(hop, moved).start()

        @pl.when(has_head & (ch < NCH))
        def _():
            def group(g, _):
                j = ch * JT + g // (CHIPS // UNROLL)
                first = (g % (CHIPS // UNROLL)) * UNROLL
                sources = [origin((first + u + 1) % CHIPS) for u in range(UNROLL)]

                @pl.when(j == ch * JT)
                def _():
                    for src in sources:
                        q_wait(src, ch)

                for src in sources:
                    attend(src, j)
                for src in sources:
                    send_o(src, j)
                return 0

            lax.fori_loop(0, JT * CHIPS // UNROLL, group, 0)

        @pl.when((ch >= LAG) & (ch < NCH + LAG))
        def _():
            done = ch - LAG

            def arrived(k, _):
                j = done * JT + k // HEADS
                h = k % HEADS
                place = orecv.at[h, pl.ds(pl.multiple_of(j * TILE, TILE), TILE)]
                pltpu.make_async_copy(obuf.at[pl.ds(0, TILE)], place,
                                      orecv_sem.at[j * HEADS + h]).wait()
                return 0

            lax.fori_loop(0, JT * HEADS, arrived, 0)
            rows = pl.ds(pl.multiple_of(done * CHUNK, CHUNK), CHUNK)
            attended = jnp.concatenate([orecv[h, rows, :] for h in range(HEADS)], axis=1)

            def project(n, _):
                cols = pl.ds(pl.multiple_of(n * NCOL, NCOL), NCOL)
                acc = jnp.dot(attended, w[:, cols], preferred_element_type=jnp.float32)
                ystage[rows, cols] = (
                    tok_cube[rows, cols].astype(jnp.float32) + gate_ref[0:1, cols] * acc
                ).astype(jnp.bfloat16)
                return 0

            lax.fori_loop(0, D // NCOL, project, 0)
            @pl.when(done < ROUND)
            def _():
                back_copy(0, done).start()

            y_copy(done).start()

            @pl.when(done >= ROUND)
            def _():
                rest_copy(done).start()


        return 0

    lax.fori_loop(0, max(NCH + LAG, ROUND + LAG + 2 * HOP), chunk_step, 0)

    order_copy().wait()

    def y_wait(ch, _):
        y_copy(ch).wait()
        rest_copy(ch).wait()

        @pl.when(ch < ROUND)
        def _():
            back_copy(1, ch).wait_send()
            back_copy(2, ch).wait_send()

        return 0

    lax.fori_loop(0, NCH, y_wait, 0)

    def drain(i, _):
        _, valid, thead = target(i)

        @pl.when(valid)
        def _():
            kv_copy(i).wait_send()
            remote(q_stage.at[thead], block(qbuf, chip, ROWS), qsend.at[thead], qrecv.at[0],
                   sibling).wait_send()
            list_copy(i).wait_send()

        return 0

    lax.fori_loop(1, CHIPS, drain, 0)

    @pl.when(has_head)
    def _():
        def drain_head(src, _):
            forward(src).wait_send()

            @pl.when(src != chip)
            def _():
                part = block(obuf, src, ROWS)
                remote(part, part, osend.at[src], orecv_sem.at[0], sibling).wait_send()

            return 0

        lax.fori_loop(0, CHIPS, drain_head, 0)


def restore(order_ref, rows_ref, out_ref, perm):
    @pl.when(pl.program_id(0) == 0)
    def _():
        perm[...] = (
            lax.broadcasted_iota(jnp.int32, (ROWS, ROWS), 0) == order_ref[...]
        ).astype(jnp.bfloat16)

    out_ref[...] = jnp.dot(perm[...], rows_ref[...],
                           preferred_element_type=jnp.float32).astype(jnp.bfloat16)


def body(tokens, queries, keyvals, out_weight, gate, cube_order, crit_owner, crit_tile, crit_count):
    live = jnp.arange(LIST, dtype=jnp.int32)[None, :] < crit_count[0][:, None]
    k_at = crit_owner[0] * (2 * QT) + crit_tile[0]
    v_at = jnp.where(live, k_at + QT, KV_TILES)
    m_at = jnp.where(live, 0, 1)

    def wide(part):
        return jnp.pad(part, ((0, 0), (0, 16 - LIST)))

    codes = jnp.concatenate([wide(k_at), wide(v_at), wide(m_at)], axis=1)
    codes = jnp.pad(codes, ((0, 0), (0, 128 - codes.shape[1])))
    bf16, i32 = jnp.bfloat16, jnp.int32
    dma = pltpu.SemaphoreType.DMA
    rows, order = pl.pallas_call(
        kernel,
        out_shape=(
            jax.ShapeDtypeStruct((ROWS, D), bf16),
            jax.ShapeDtypeStruct((1, ROWS), i32),
        ),
        in_specs=[pl.BlockSpec(memory_space=pl.ANY)] * 4
        + [pl.BlockSpec(memory_space=pltpu.VMEM)] * 3,
        out_specs=(
            pl.BlockSpec(memory_space=pl.ANY),
            pl.BlockSpec(memory_space=pl.ANY),
        ),
        scratch_shapes=[
            pltpu.VMEM((ROWS, D), bf16),
            pltpu.VMEM((ROWS, HW), bf16),
            pltpu.VMEM((ROWS, 2, HW), bf16),
            pltpu.VMEM((HW, D), bf16),
            pltpu.VMEM((ROWS, ROWS), bf16),
            pltpu.VMEM((ROWS, D), bf16),
            pltpu.VMEM((HEADS, 2 * QT, TILE, HEAD_DIM), bf16),
            pltpu.VMEM((HEADS, ROWS, HEAD_DIM), bf16),
            pltpu.VMEM((KV_TILES + 1, TILE, HEAD_DIM), bf16),
            pltpu.VMEM((CHIPS * ROWS, HEAD_DIM), bf16),
            pltpu.VMEM((CHIPS * ROWS, HEAD_DIM), bf16),
            pltpu.VMEM((2, TILE, HEAD_DIM), bf16),
            pltpu.VMEM((CHIPS * QT, 128), i32),
            pltpu.SMEM((CHIPS * QT, 128), i32),
            pltpu.VMEM((HEADS, ROWS, HEAD_DIM), bf16),
            pltpu.VMEM((ROWS, D), bf16),
            pltpu.VMEM((2, ROWS, D - Y_COLS), bf16),
            dma((4,)), dma, dma((HEADS,)), dma((CHIPS,)), dma((CHIPS,)), dma((CHIPS,)),
            dma((HEADS,)), dma((CHIPS * NCH,)), dma((HEADS,)), dma((CHIPS,)),
            dma((CHIPS,)), dma((QT * HEADS,)), dma((NCH,)), dma((NCH,)), dma((3, NCH)), dma((3, NCH)),
            dma, dma,
        ],
        compiler_params=pltpu.CompilerParams(
            collective_id=0, has_side_effects=True, vmem_limit_bytes=60 * 2**20
        ),
        cost_estimate=pl.CostEstimate(
            flops=16 * 10**9, bytes_accessed=22 * 2**20, transcendentals=10**7
        ),
        name="cube_attention",
    )(tokens[0], queries[0], keyvals[0], out_weight[0], gate, cube_order[0], codes)
    handed = pl.pallas_call(
        restore,
        out_shape=jax.ShapeDtypeStruct((ROWS, D), bf16),
        grid=(D // R_COLS,),
        in_specs=[
            pl.BlockSpec((1, ROWS), lambda n: (0, 0)),
            pl.BlockSpec((ROWS, R_COLS), lambda n: (0, n)),
        ],
        out_specs=pl.BlockSpec((ROWS, R_COLS), lambda n: (0, n)),
        scratch_shapes=[pltpu.VMEM((ROWS, ROWS), bf16)],
        name="token_order",
    )(order, rows)
    return handed[None]


def solution(mesh):
    in_specs = (
        P("section", "ctx", None),
        P("section", "ctx", None),
        P("section", "ctx", None, None),
        P("section", None, None),
        P("section", None),
        P("section", "ctx", None),
        P("section", "ctx", None),
        P("section", "ctx", None),
        P("section", "ctx"),
    )
    out_specs = P("section", "ctx", None)
    return jax.shard_map(body, mesh=mesh, in_specs=in_specs, out_specs=out_specs, check_vma=False)
```

```python
import math

import jax
import jax.numpy as jnp
from jax import lax
from jax.experimental import pallas as pl
from jax.experimental.pallas import tpu as pltpu
from jax.sharding import PartitionSpec as P

D = 3072
HEADS = 12
HEAD_DIM = 128
TILE = 64
LIST = 12
QT = 8
HW = 1536
ROWS = 512
CTX = 32
SIDE = 4
CHIPS = 16
SECTIONS = 4
KV_TILES = CTX * 2 * QT
JT = 1
CHUNK = JT * TILE
NCH = QT // JT
UNROLL = 8
Q_FIRST = 1
LAG = 1
HOP = 2
Y_COLS = 2304
ROUND = 7
NCOL = 512
R_COLS = 1024
EXP_SCALE = math.log2(math.e) / math.sqrt(HEAD_DIM)


def kernel(
    tok_hbm, q_hbm, kv_hbm, w_hbm, gate_ref, order_ref, codes_ref, yrecv, prev_order,
    tok, q_in, kv_in, w, perm, tok_cube, kv_stage, q_stage, kvbuf, qbuf, obuf, ones,
    lists, lists_smem, orecv, ystage, relay,
    load_sem, smem_sem, ksend, krecv, fsend, frecv, qsend, qrecv, lsend, lrecv,
    osend, orecv_sem, ysend, yrecv_sem, bsend, brecv, psend, precv,
):
    sec = lax.axis_index("section")
    me = lax.axis_index("ctx")
    core = me % 2
    chip = me // 2
    cx, cz = chip // SIDE, chip % SIDE
    kind = (cz - cx + 3) % SIDE
    has_head = kind < 3
    head = cx + SIDE * kind
    sibling = (sec, me + 1 - 2 * core)
    ahead = ((sec + 1) % SECTIONS, me)
    behind = ((sec + SECTIONS - 1) % SECTIONS, me)

    def remote(src, dst, send, recv, device):
        return pltpu.make_async_remote_copy(
            src_ref=src, dst_ref=dst, send_sem=send, recv_sem=recv,
            device_id=device, device_id_type=pl.DeviceIdType.MESH,
        )

    def load(i):
        src = (kv_hbm, q_hbm, tok_hbm, w_hbm)[i]
        return pltpu.make_async_copy(src, (kv_in, q_in, tok, w)[i], load_sem.at[i])

    load(0).start()

    barrier = pltpu.get_barrier_semaphore()

    def greet(i, _):
        other = (chip + i) % CHIPS
        pl.semaphore_signal(barrier, inc=1, device_id=(sec, 2 * other + core),
                            device_id_type=pl.DeviceIdType.MESH)
        return 0

    lax.fori_loop(1, CHIPS, greet, 0)
    for device in (sibling, ahead, behind):
        pl.semaphore_signal(barrier, inc=1, device_id=device,
                            device_id_type=pl.DeviceIdType.MESH)

    column = jnp.transpose(jnp.broadcast_to(order_ref[...], (128, ROWS)))[:, :1]
    perm[...] = (lax.broadcasted_iota(jnp.int32, (ROWS, ROWS), 1) == column).astype(jnp.bfloat16)
    ones[0] = jnp.ones((TILE, HEAD_DIM), jnp.bfloat16)
    ones[1] = jnp.zeros((TILE, HEAD_DIM), jnp.bfloat16)
    kvbuf[KV_TILES] = jnp.zeros((TILE, HEAD_DIM), jnp.bfloat16)

    pl.semaphore_wait(barrier, CHIPS + 2)

    def order_copy():
        return remote(order_ref, prev_order, psend, precv, ahead)

    order_copy().start()

    def shift(i):
        dx, dz = i % SIDE, (i // SIDE + 3 * (i % SIDE)) % SIDE
        return dx + core * (dz - dx), dz + core * (dx - dz)

    def target(i):
        dx, dz = shift(i)
        tx, tz = (cx + dx) % SIDE, (cz + dz) % SIDE
        tkind = (tz - tx + 3) % SIDE
        return tx * SIDE + tz, tkind < 3, tx + SIDE * tkind

    def origin(i):
        dx, dz = shift(i)
        return ((cx + SIDE - dx) % SIDE) * SIDE + (cz + SIDE - dz) % SIDE

    def block(ref, index, rows):
        return ref.at[pl.ds(pl.multiple_of(index * rows, rows), rows)]

    def list_copy(i):
        to, _, thead = target(i)
        return remote(codes_ref, block(lists, chip, QT), lsend.at[thead], lrecv.at[chip],
                      (sec, 2 * to + core))

    def kv_copy(i):
        to, _, thead = target(i)
        return remote(kv_stage.at[thead], block(kvbuf, me, 2 * QT), ksend.at[thead],
                      krecv.at[chip], (sec, 2 * to + core))

    def q_rows(src, ch):
        return pl.ds(pl.multiple_of(src * ROWS + ch * CHUNK, CHUNK), CHUNK)

    def q_copy(i, ch):
        to, _, thead = target(i)
        rows = pl.ds(pl.multiple_of(ch * CHUNK, CHUNK), CHUNK)
        return remote(q_stage.at[thead, rows], qbuf.at[q_rows(chip, ch)], qsend.at[thead],
                      qrecv.at[chip * NCH + ch], (sec, 2 * to + core))

    def forward(from_chip):
        part = block(kvbuf, 2 * from_chip + core, 2 * QT)
        return remote(part, part, fsend.at[from_chip], frecv.at[from_chip], sibling)

    def lanes(h):
        return pl.ds(pl.multiple_of(h * HEAD_DIM, HEAD_DIM), HEAD_DIM)

    def cube_pairs(h):
        both = jnp.concatenate([kv_in[:, 0, lanes(h)], kv_in[:, 1, lanes(h)]], axis=1)
        rows = jnp.dot(perm[...], both, preferred_element_type=jnp.float32).astype(jnp.bfloat16)
        rows = rows.reshape(QT, TILE, 2 * HEAD_DIM)
        return rows[:, :, :HEAD_DIM], rows[:, :, HEAD_DIM:]

    def cube_query(h):
        return jnp.dot(perm[...], q_in[:, lanes(h)],
                       preferred_element_type=jnp.float32).astype(jnp.bfloat16)

    load(0).wait()
    for i in range(1, 4):
        load(i).start()

    def send_kv(i, _):
        _, valid, thead = target(i)

        @pl.when(valid)
        def _():
            keys, values = cube_pairs(thead)
            kv_stage[thead, 0:QT] = keys
            kv_stage[thead, QT:] = values
            kv_copy(i).start()
            list_copy(i).start()

        return 0

    lax.fori_loop(1, CHIPS, send_kv, 0)

    @pl.when(has_head)
    def _():
        keys, values = cube_pairs(head)
        kvbuf[pl.ds(me * 2 * QT, QT)] = keys
        kvbuf[pl.ds(me * 2 * QT + QT, QT)] = values
        forward(chip).start()
        lists[pl.ds(pl.multiple_of(chip * QT, QT), QT)] = codes_ref[...]

    load(1).wait()

    def make_q(i, _):
        _, valid, thead = target(i)

        @pl.when(valid)
        def _():
            q_stage[thead] = cube_query(thead)

        return 0

    lax.fori_loop(1, CHIPS, make_q, 0)

    def send_q(ch):
        def one(i, _):
            _, valid, _ = target(i)

            @pl.when(valid)
            def _():
                q_copy(i, ch).start()

            return 0

        lax.fori_loop(1, CHIPS, one, 0)

    for ch in range(Q_FIRST):
        send_q(ch)

    @pl.when(has_head)
    def _():
        qbuf[pl.ds(pl.multiple_of(chip * ROWS, ROWS), ROWS)] = cube_query(head)

    load(2).wait()

    def cube_tokens(n, _):
        cols = pl.ds(pl.multiple_of(n * NCOL, NCOL), NCOL)
        tok_cube[:, cols] = jnp.dot(perm[...], tok[:, cols],
                                    preferred_element_type=jnp.float32).astype(jnp.bfloat16)
        return 0

    lax.fori_loop(0, D // NCOL, cube_tokens, 0)

    @pl.when(has_head)
    def _():
        def pass_on(i, _):
            src = origin(i)
            remote(kv_stage.at[0], block(kvbuf, 2 * src + core, 2 * QT), ksend.at[0],
                   krecv.at[src], sibling).wait_recv()
            forward(src).start()
            return 0

        lax.fori_loop(1, CHIPS, pass_on, 0)

        def small(i, _):
            src = origin(i)
            remote(codes_ref, block(lists, src, QT), lsend.at[0], lrecv.at[src],
                   sibling).wait_recv()
            return 0

        lax.fori_loop(1, CHIPS, small, 0)

        to_smem = pltpu.make_async_copy(lists, lists_smem, smem_sem)
        to_smem.start()

        def passed(src, _):
            part = block(kvbuf, 2 * src + 1 - core, 2 * QT)
            remote(part, part, fsend.at[src], frecv.at[src], sibling).wait_recv()
            return 0

        lax.fori_loop(0, CHIPS, passed, 0)
        to_smem.wait()

    load(3).wait()

    def o_rows(src, j):
        return pl.ds(pl.multiple_of(src * ROWS + j * TILE, TILE), TILE)

    def attend(src, j):
        q = qbuf[o_rows(src, j), :]
        row = src * QT + j
        ks, vs, marks = [], [], []
        for e in range(LIST):
            ks.append(kvbuf[lists_smem[row, e]])
            vs.append(kvbuf[lists_smem[row, 16 + e]])
            marks.append(ones[lists_smem[row, 32 + e]])
        scores = lax.dot_general(q, jnp.concatenate(ks, 0), (((1,), (1,)), ((), ())),
                                 preferred_element_type=jnp.float32)
        top = jnp.max(scores, axis=-1, keepdims=True)
        weights = jnp.exp2((scores - top) * EXP_SCALE).astype(jnp.bfloat16)
        sums = jnp.concatenate([jnp.concatenate(vs, 0), jnp.concatenate(marks, 0)], 1)
        both = jnp.dot(weights, sums, preferred_element_type=jnp.float32)
        obuf[o_rows(src, j), :] = (both[:, :HEAD_DIM] / both[:, HEAD_DIM:]).astype(jnp.bfloat16)

    def send_o(src, j):
        part = obuf.at[o_rows(src, j)]
        place = orecv.at[head, pl.ds(pl.multiple_of(j * TILE, TILE), TILE)]
        sem = orecv_sem.at[j * HEADS + head]

        @pl.when(src != chip)
        def _():
            remote(part, place, osend.at[src], sem, (sec, 2 * src + core)).start()

        @pl.when(src == chip)
        def _():
            pltpu.make_async_copy(part, place, sem).start()

    def y_copy(ch):
        rows = pl.ds(pl.multiple_of(ch * CHUNK, CHUNK), CHUNK)
        cols = pl.ds(0, Y_COLS)
        return remote(ystage.at[rows, cols], yrecv.at[rows, cols], ysend.at[ch],
                      yrecv_sem.at[ch], ahead)

    def rest_copy(ch):
        rows = pl.ds(pl.multiple_of(ch * CHUNK, CHUNK), CHUNK)
        cols = pl.ds(Y_COLS, D - Y_COLS)
        return remote(ystage.at[rows, cols], yrecv.at[rows, cols], bsend.at[0, ch],
                      brecv.at[2, ch], ahead)

    def back_copy(hop, ch):
        rows = pl.ds(pl.multiple_of(ch * CHUNK, CHUNK), CHUNK)
        cols = pl.ds(Y_COLS, D - Y_COLS)
        if hop == 0:
            src, dst = ystage.at[rows, cols], relay.at[0, rows]
        elif hop == 1:
            src, dst = relay.at[0, rows], relay.at[1, rows]
        else:
            src, dst = relay.at[1, rows], yrecv.at[rows, cols]
        return remote(src, dst, bsend.at[hop, ch], brecv.at[hop, ch], behind)

    def q_wait(src, ch):
        @pl.when(src != chip)
        def _():
            remote(q_stage.at[0, pl.ds(0, CHUNK)], qbuf.at[q_rows(src, ch)], qsend.at[0],
                   qrecv.at[src * NCH + ch], sibling).wait_recv()

    def chunk_step(ch, _):
        @pl.when(ch + Q_FIRST < NCH)
        def _():
            send_q(ch + Q_FIRST)

        for hop in (2, 1):
            moved = ch - LAG - HOP * hop

            @pl.when((moved >= 0) & (moved < ROUND))
            def _():
                back_copy(hop - 1, moved).wait_recv()
                back_copy(hop, moved).start()

        @pl.when(has_head & (ch < NCH))
        def _():
            def group(g, _):
                j = ch * JT + g // (CHIPS // UNROLL)
                first = (g % (CHIPS // UNROLL)) * UNROLL
                sources = [origin((first + u + 1) % CHIPS) for u in range(UNROLL)]

                @pl.when(j == ch * JT)
                def _():
                    for src in sources:
                        q_wait(src, ch)

                for src in sources:
                    attend(src, j)
                for src in sources:
                    send_o(src, j)
                return 0

            lax.fori_loop(0, JT * CHIPS // UNROLL, group, 0)

        @pl.when((ch >= LAG) & (ch < NCH + LAG))
        def _():
            done = ch - LAG

            def arrived(k, _):
                j = done * JT + k // HEADS
                h = k % HEADS
                place = orecv.at[h, pl.ds(pl.multiple_of(j * TILE, TILE), TILE)]
                pltpu.make_async_copy(obuf.at[pl.ds(0, TILE)], place,
                                      orecv_sem.at[j * HEADS + h]).wait()
                return 0

            lax.fori_loop(0, JT * HEADS, arrived, 0)
            rows = pl.ds(pl.multiple_of(done * CHUNK, CHUNK), CHUNK)
            attended = jnp.concatenate([orecv[h, rows, :] for h in range(HEADS)], axis=1)

            def project(n, _):
                cols = pl.ds(pl.multiple_of(n * NCOL, NCOL), NCOL)
                acc = jnp.dot(attended, w[:, cols], preferred_element_type=jnp.float32)
                ystage[rows, cols] = (
                    tok_cube[rows, cols].astype(jnp.float32) + gate_ref[0:1, cols] * acc
                ).astype(jnp.bfloat16)
                return 0

            lax.fori_loop(0, D // NCOL, project, 0)
            @pl.when(done < ROUND)
            def _():
                back_copy(0, done).start()

            y_copy(done).start()

            @pl.when(done >= ROUND)
            def _():
                rest_copy(done).start()


        return 0

    lax.fori_loop(0, max(NCH + LAG, ROUND + LAG + 2 * HOP), chunk_step, 0)

    order_copy().wait()

    def y_wait(ch, _):
        y_copy(ch).wait()
        rest_copy(ch).wait()

        @pl.when(ch < ROUND)
        def _():
            back_copy(1, ch).wait_send()
            back_copy(2, ch).wait_send()

        return 0

    lax.fori_loop(0, NCH, y_wait, 0)

    def drain(i, _):
        _, valid, thead = target(i)

        @pl.when(valid)
        def _():
            kv_copy(i).wait_send()
            remote(q_stage.at[thead], block(qbuf, chip, ROWS), qsend.at[thead], qrecv.at[0],
                   sibling).wait_send()
            list_copy(i).wait_send()

        return 0

    lax.fori_loop(1, CHIPS, drain, 0)

    @pl.when(has_head)
    def _():
        def drain_head(src, _):
            forward(src).wait_send()

            @pl.when(src != chip)
            def _():
                part = block(obuf, src, ROWS)
                remote(part, part, osend.at[src], orecv_sem.at[0], sibling).wait_send()

            return 0

        lax.fori_loop(0, CHIPS, drain_head, 0)


def restore(order_ref, rows_ref, out_ref, perm):
    @pl.when(pl.program_id(0) == 0)
    def _():
        perm[...] = (
            lax.broadcasted_iota(jnp.int32, (ROWS, ROWS), 0) == order_ref[...]
        ).astype(jnp.bfloat16)

    out_ref[...] = jnp.dot(perm[...], rows_ref[...],
                           preferred_element_type=jnp.float32).astype(jnp.bfloat16)


def body(tokens, queries, keyvals, out_weight, gate, cube_order, crit_owner, crit_tile, crit_count):
    live = jnp.arange(LIST, dtype=jnp.int32)[None, :] < crit_count[0][:, None]
    k_at = crit_owner[0] * (2 * QT) + crit_tile[0]
    v_at = jnp.where(live, k_at + QT, KV_TILES)
    m_at = jnp.where(live, 0, 1)

    def wide(part):
        return jnp.pad(part, ((0, 0), (0, 16 - LIST)))

    codes = jnp.concatenate([wide(k_at), wide(v_at), wide(m_at)], axis=1)
    codes = jnp.pad(codes, ((0, 0), (0, 128 - codes.shape[1])))
    bf16, i32 = jnp.bfloat16, jnp.int32
    dma = pltpu.SemaphoreType.DMA
    rows, order = pl.pallas_call(
        kernel,
        out_shape=(
            jax.ShapeDtypeStruct((ROWS, D), bf16),
            jax.ShapeDtypeStruct((1, ROWS), i32),
        ),
        in_specs=[pl.BlockSpec(memory_space=pl.ANY)] * 4
        + [pl.BlockSpec(memory_space=pltpu.VMEM)] * 3,
        out_specs=(
            pl.BlockSpec(memory_space=pl.ANY),
            pl.BlockSpec(memory_space=pl.ANY),
        ),
        scratch_shapes=[
            pltpu.VMEM((ROWS, D), bf16),
            pltpu.VMEM((ROWS, HW), bf16),
            pltpu.VMEM((ROWS, 2, HW), bf16),
            pltpu.VMEM((HW, D), bf16),
            pltpu.VMEM((ROWS, ROWS), bf16),
            pltpu.VMEM((ROWS, D), bf16),
            pltpu.VMEM((HEADS, 2 * QT, TILE, HEAD_DIM), bf16),
            pltpu.VMEM((HEADS, ROWS, HEAD_DIM), bf16),
            pltpu.VMEM((KV_TILES + 1, TILE, HEAD_DIM), bf16),
            pltpu.VMEM((CHIPS * ROWS, HEAD_DIM), bf16),
            pltpu.VMEM((CHIPS * ROWS, HEAD_DIM), bf16),
            pltpu.VMEM((2, TILE, HEAD_DIM), bf16),
            pltpu.VMEM((CHIPS * QT, 128), i32),
            pltpu.SMEM((CHIPS * QT, 128), i32),
            pltpu.VMEM((HEADS, ROWS, HEAD_DIM), bf16),
            pltpu.VMEM((ROWS, D), bf16),
            pltpu.VMEM((2, ROWS, D - Y_COLS), bf16),
            dma((4,)), dma, dma((HEADS,)), dma((CHIPS,)), dma((CHIPS,)), dma((CHIPS,)),
            dma((HEADS,)), dma((CHIPS * NCH,)), dma((HEADS,)), dma((CHIPS,)),
            dma((CHIPS,)), dma((QT * HEADS,)), dma((NCH,)), dma((NCH,)), dma((3, NCH)), dma((3, NCH)),
            dma, dma,
        ],
        compiler_params=pltpu.CompilerParams(
            collective_id=0, has_side_effects=True, vmem_limit_bytes=60 * 2**20
        ),
        cost_estimate=pl.CostEstimate(
            flops=16 * 10**9, bytes_accessed=22 * 2**20, transcendentals=10**7
        ),
        name="cube_attention",
    )(tokens[0], queries[0], keyvals[0], out_weight[0], gate, cube_order[0], codes)
    handed = pl.pallas_call(
        restore,
        out_shape=jax.ShapeDtypeStruct((ROWS, D), bf16),
        grid=(D // R_COLS,),
        in_specs=[
            pl.BlockSpec((1, ROWS), lambda n: (0, 0)),
            pl.BlockSpec((ROWS, R_COLS), lambda n: (0, n)),
        ],
        out_specs=pl.BlockSpec((ROWS, R_COLS), lambda n: (0, n)),
        scratch_shapes=[pltpu.VMEM((ROWS, ROWS), bf16)],
        name="token_order",
    )(order, rows)
    return handed[None]


def solution(mesh):
    in_specs = (
        P("section", "ctx", None),
        P("section", "ctx", None),
        P("section", "ctx", None, None),
        P("section", None, None),
        P("section", None),
        P("section", "ctx", None),
        P("section", "ctx", None),
        P("section", "ctx", None),
        P("section", "ctx"),
    )
    out_specs = P("section", "ctx", None)
    return jax.shard_map(body, mesh=mesh, in_specs=in_specs, out_specs=out_specs, check_vma=False)
```

```python
import math

import jax
import jax.numpy as jnp
from jax import lax
from jax.experimental import pallas as pl
from jax.experimental.pallas import tpu as pltpu
from jax.sharding import PartitionSpec as P

D = 3072
HEADS = 12
HEAD_DIM = 128
TILE = 64
LIST = 12
QT = 8
HW = 1536
ROWS = 512
CTX = 32
SIDE = 4
CHIPS = 16
SECTIONS = 4
KV_TILES = CTX * 2 * QT
JT = 1
CHUNK = JT * TILE
NCH = QT // JT
UNROLL = 8
Q_FIRST = 1
LAG = 1
HOP = 2
Y_COLS = 2304
P_COLS = D - Y_COLS
AHEAD = Y_COLS // P_COLS
ROUND = 7
NCOL = 512
R_COLS = 1024
EXP_SCALE = math.log2(math.e) / math.sqrt(HEAD_DIM)


def kernel(
    tok_hbm, q_hbm, kv_hbm, w_hbm, gate_ref, order_ref, codes_ref, yrecv, prev_order,
    tok, q_in, kv_in, w, perm, tok_cube, kv_stage, q_stage, kvbuf, qbuf, obuf, ones,
    lists, lists_smem, orecv, ystage, relay,
    load_sem, smem_sem, ksend, krecv, fsend, frecv, qsend, qrecv, lsend, lrecv,
    osend, orecv_sem, ysend, yrecv_sem, bsend, brecv, psend, precv,
):
    sec = lax.axis_index("section")
    me = lax.axis_index("ctx")
    core = me % 2
    chip = me // 2
    cx, cz = chip // SIDE, chip % SIDE
    kind = (cz - cx + 3) % SIDE
    has_head = kind < 3
    head = cx + SIDE * kind
    sibling = (sec, me + 1 - 2 * core)
    ahead = ((sec + 1) % SECTIONS, me)
    behind = ((sec + SECTIONS - 1) % SECTIONS, me)

    def remote(src, dst, send, recv, device):
        return pltpu.make_async_remote_copy(
            src_ref=src, dst_ref=dst, send_sem=send, recv_sem=recv,
            device_id=device, device_id_type=pl.DeviceIdType.MESH,
        )

    def load(i):
        src = (kv_hbm, q_hbm, tok_hbm, w_hbm)[i]
        return pltpu.make_async_copy(src, (kv_in, q_in, tok, w)[i], load_sem.at[i])

    load(0).start()

    barrier = pltpu.get_barrier_semaphore()

    def greet(i, _):
        other = (chip + i) % CHIPS
        pl.semaphore_signal(barrier, inc=1, device_id=(sec, 2 * other + core),
                            device_id_type=pl.DeviceIdType.MESH)
        return 0

    lax.fori_loop(1, CHIPS, greet, 0)
    for device in (sibling, ahead, behind):
        pl.semaphore_signal(barrier, inc=1, device_id=device,
                            device_id_type=pl.DeviceIdType.MESH)

    column = jnp.transpose(jnp.broadcast_to(order_ref[...], (128, ROWS)))[:, :1]
    perm[...] = (lax.broadcasted_iota(jnp.int32, (ROWS, ROWS), 1) == column).astype(jnp.bfloat16)
    ones[0] = jnp.ones((TILE, HEAD_DIM), jnp.bfloat16)
    ones[1] = jnp.zeros((TILE, HEAD_DIM), jnp.bfloat16)
    kvbuf[KV_TILES] = jnp.zeros((TILE, HEAD_DIM), jnp.bfloat16)

    pl.semaphore_wait(barrier, CHIPS + 2)

    def order_copy():
        return remote(order_ref, prev_order, psend, precv, ahead)

    order_copy().start()

    def shift(i):
        dx, dz = i % SIDE, (i // SIDE + 3 * (i % SIDE)) % SIDE
        return dx + core * (dz - dx), dz + core * (dx - dz)

    def target(i):
        dx, dz = shift(i)
        tx, tz = (cx + dx) % SIDE, (cz + dz) % SIDE
        tkind = (tz - tx + 3) % SIDE
        return tx * SIDE + tz, tkind < 3, tx + SIDE * tkind

    def origin(i):
        dx, dz = shift(i)
        return ((cx + SIDE - dx) % SIDE) * SIDE + (cz + SIDE - dz) % SIDE

    def block(ref, index, rows):
        return ref.at[pl.ds(pl.multiple_of(index * rows, rows), rows)]

    def list_copy(i):
        to, _, thead = target(i)
        return remote(codes_ref, block(lists, chip, QT), lsend.at[thead], lrecv.at[chip],
                      (sec, 2 * to + core))

    def kv_copy(i):
        to, _, thead = target(i)
        return remote(kv_stage.at[thead], block(kvbuf, me, 2 * QT), ksend.at[thead],
                      krecv.at[chip], (sec, 2 * to + core))

    def q_rows(src, ch):
        return pl.ds(pl.multiple_of(src * ROWS + ch * CHUNK, CHUNK), CHUNK)

    def q_copy(i, ch):
        to, _, thead = target(i)
        rows = pl.ds(pl.multiple_of(ch * CHUNK, CHUNK), CHUNK)
        return remote(q_stage.at[thead, rows], qbuf.at[q_rows(chip, ch)], qsend.at[thead],
                      qrecv.at[chip * NCH + ch], (sec, 2 * to + core))

    def forward(from_chip):
        part = block(kvbuf, 2 * from_chip + core, 2 * QT)
        return remote(part, part, fsend.at[from_chip], frecv.at[from_chip], sibling)

    def lanes(h):
        return pl.ds(pl.multiple_of(h * HEAD_DIM, HEAD_DIM), HEAD_DIM)

    def cube_pairs(h):
        both = jnp.concatenate([kv_in[:, 0, lanes(h)], kv_in[:, 1, lanes(h)]], axis=1)
        rows = jnp.dot(perm[...], both, preferred_element_type=jnp.float32).astype(jnp.bfloat16)
        rows = rows.reshape(QT, TILE, 2 * HEAD_DIM)
        return rows[:, :, :HEAD_DIM], rows[:, :, HEAD_DIM:]

    def cube_query(h):
        return jnp.dot(perm[...], q_in[:, lanes(h)],
                       preferred_element_type=jnp.float32).astype(jnp.bfloat16)

    load(0).wait()
    for i in range(1, 4):
        load(i).start()

    def send_kv(i, _):
        _, valid, thead = target(i)

        @pl.when(valid)
        def _():
            keys, values = cube_pairs(thead)
            kv_stage[thead, 0:QT] = keys
            kv_stage[thead, QT:] = values
            kv_copy(i).start()
            list_copy(i).start()

        return 0

    lax.fori_loop(1, CHIPS, send_kv, 0)

    @pl.when(has_head)
    def _():
        keys, values = cube_pairs(head)
        kvbuf[pl.ds(me * 2 * QT, QT)] = keys
        kvbuf[pl.ds(me * 2 * QT + QT, QT)] = values
        forward(chip).start()
        lists[pl.ds(pl.multiple_of(chip * QT, QT), QT)] = codes_ref[...]

    load(1).wait()

    def make_q(i, _):
        _, valid, thead = target(i)

        @pl.when(valid)
        def _():
            q_stage[thead] = cube_query(thead)

        return 0

    lax.fori_loop(1, CHIPS, make_q, 0)

    def send_q(ch):
        def one(i, _):
            _, valid, _ = target(i)

            @pl.when(valid)
            def _():
                q_copy(i, ch).start()

            return 0

        lax.fori_loop(1, CHIPS, one, 0)

    for ch in range(Q_FIRST):
        send_q(ch)

    @pl.when(has_head)
    def _():
        qbuf[pl.ds(pl.multiple_of(chip * ROWS, ROWS), ROWS)] = cube_query(head)

    load(2).wait()

    def cube_tokens(n, _):
        cols = pl.ds(pl.multiple_of(n * NCOL, NCOL), NCOL)
        tok_cube[:, cols] = jnp.dot(perm[...], tok[:, cols],
                                    preferred_element_type=jnp.float32).astype(jnp.bfloat16)
        return 0

    lax.fori_loop(0, D // NCOL, cube_tokens, 0)

    @pl.when(has_head)
    def _():
        def pass_on(i, _):
            src = origin(i)
            remote(kv_stage.at[0], block(kvbuf, 2 * src + core, 2 * QT), ksend.at[0],
                   krecv.at[src], sibling).wait_recv()
            forward(src).start()
            return 0

        lax.fori_loop(1, CHIPS, pass_on, 0)

        def small(i, _):
            src = origin(i)
            remote(codes_ref, block(lists, src, QT), lsend.at[0], lrecv.at[src],
                   sibling).wait_recv()
            return 0

        lax.fori_loop(1, CHIPS, small, 0)

        to_smem = pltpu.make_async_copy(lists, lists_smem, smem_sem)
        to_smem.start()

        def passed(src, _):
            part = block(kvbuf, 2 * src + 1 - core, 2 * QT)
            remote(part, part, fsend.at[src], frecv.at[src], sibling).wait_recv()
            return 0

        lax.fori_loop(0, CHIPS, passed, 0)
        to_smem.wait()

    load(3).wait()

    def o_rows(src, j):
        return pl.ds(pl.multiple_of(src * ROWS + j * TILE, TILE), TILE)

    def attend(src, j):
        q = qbuf[o_rows(src, j), :]
        row = src * QT + j
        ks, vs, marks = [], [], []
        for e in range(LIST):
            ks.append(kvbuf[lists_smem[row, e]])
            vs.append(kvbuf[lists_smem[row, 16 + e]])
            marks.append(ones[lists_smem[row, 32 + e]])
        scores = lax.dot_general(q, jnp.concatenate(ks, 0), (((1,), (1,)), ((), ())),
                                 preferred_element_type=jnp.float32)
        top = jnp.max(scores, axis=-1, keepdims=True)
        weights = jnp.exp2((scores - top) * EXP_SCALE).astype(jnp.bfloat16)
        sums = jnp.concatenate([jnp.concatenate(vs, 0), jnp.concatenate(marks, 0)], 1)
        both = jnp.dot(weights, sums, preferred_element_type=jnp.float32)
        obuf[o_rows(src, j), :] = (both[:, :HEAD_DIM] / both[:, HEAD_DIM:]).astype(jnp.bfloat16)

    def send_o(src, j):
        part = obuf.at[o_rows(src, j)]
        place = orecv.at[head, pl.ds(pl.multiple_of(j * TILE, TILE), TILE)]
        sem = orecv_sem.at[j * HEADS + head]

        @pl.when(src != chip)
        def _():
            remote(part, place, osend.at[src], sem, (sec, 2 * src + core)).start()

        @pl.when(src == chip)
        def _():
            pltpu.make_async_copy(part, place, sem).start()

    def y_copy(ch, n):
        rows = pl.ds(pl.multiple_of(ch * CHUNK, CHUNK), CHUNK)
        cols = pl.ds(pl.multiple_of(n * P_COLS, P_COLS), P_COLS)
        return remote(ystage.at[rows, cols], yrecv.at[rows, cols], ysend.at[n, ch],
                      yrecv_sem.at[n, ch], ahead)

    def rest_copy(ch):
        rows = pl.ds(pl.multiple_of(ch * CHUNK, CHUNK), CHUNK)
        cols = pl.ds(Y_COLS, D - Y_COLS)
        return remote(ystage.at[rows, cols], yrecv.at[rows, cols], bsend.at[0, ch],
                      brecv.at[2, ch], ahead)

    def back_copy(hop, ch):
        rows = pl.ds(pl.multiple_of(ch * CHUNK, CHUNK), CHUNK)
        cols = pl.ds(Y_COLS, D - Y_COLS)
        if hop == 0:
            src, dst = ystage.at[rows, cols], relay.at[0, rows]
        elif hop == 1:
            src, dst = relay.at[0, rows], relay.at[1, rows]
        else:
            src, dst = relay.at[1, rows], yrecv.at[rows, cols]
        return remote(src, dst, bsend.at[hop, ch], brecv.at[hop, ch], behind)

    def q_wait(src, ch):
        @pl.when(src != chip)
        def _():
            remote(q_stage.at[0, pl.ds(0, CHUNK)], qbuf.at[q_rows(src, ch)], qsend.at[0],
                   qrecv.at[src * NCH + ch], sibling).wait_recv()

    def chunk_step(ch, _):
        @pl.when(ch + Q_FIRST < NCH)
        def _():
            send_q(ch + Q_FIRST)

        for hop in (2, 1):
            moved = ch - LAG - HOP * hop

            @pl.when((moved >= 0) & (moved < ROUND))
            def _():
                back_copy(hop - 1, moved).wait_recv()
                back_copy(hop, moved).start()

        @pl.when(has_head & (ch < NCH))
        def _():
            def group(g, _):
                j = ch * JT + g // (CHIPS // UNROLL)
                first = (g % (CHIPS // UNROLL)) * UNROLL
                sources = [origin((first + u + 1) % CHIPS) for u in range(UNROLL)]

                @pl.when(j == ch * JT)
                def _():
                    for src in sources:
                        q_wait(src, ch)

                for src in sources:
                    attend(src, j)
                for src in sources:
                    send_o(src, j)
                return 0

            lax.fori_loop(0, JT * CHIPS // UNROLL, group, 0)

        @pl.when((ch >= LAG) & (ch < NCH + LAG))
        def _():
            done = ch - LAG

            def arrived(k, _):
                j = done * JT + k // HEADS
                h = k % HEADS
                place = orecv.at[h, pl.ds(pl.multiple_of(j * TILE, TILE), TILE)]
                pltpu.make_async_copy(obuf.at[pl.ds(0, TILE)], place,
                                      orecv_sem.at[j * HEADS + h]).wait()
                return 0

            lax.fori_loop(0, JT * HEADS, arrived, 0)
            rows = pl.ds(pl.multiple_of(done * CHUNK, CHUNK), CHUNK)
            attended = jnp.concatenate([orecv[h, rows, :] for h in range(HEADS)], axis=1)

            def project(k, _):
                n = (k + AHEAD) % (AHEAD + 1)
                cols = pl.ds(pl.multiple_of(n * P_COLS, P_COLS), P_COLS)
                acc = jnp.dot(attended, w[:, cols], preferred_element_type=jnp.float32)
                ystage[rows, cols] = (
                    tok_cube[rows, cols].astype(jnp.float32) + gate_ref[0:1, cols] * acc
                ).astype(jnp.bfloat16)

                @pl.when((k == 0) & (done < ROUND))
                def _():
                    back_copy(0, done).start()

                @pl.when((k == 0) & (done >= ROUND))
                def _():
                    rest_copy(done).start()

                @pl.when(k > 0)
                def _():
                    y_copy(done, n).start()

                return 0

            lax.fori_loop(0, AHEAD + 1, project, 0)

        return 0

    lax.fori_loop(0, max(NCH + LAG, ROUND + LAG + 2 * HOP), chunk_step, 0)

    order_copy().wait()

    def y_wait(ch, _):
        for n in range(AHEAD):
            y_copy(ch, n).wait()
        rest_copy(ch).wait()

        @pl.when(ch < ROUND)
        def _():
            back_copy(1, ch).wait_send()
            back_copy(2, ch).wait_send()

        return 0

    lax.fori_loop(0, NCH, y_wait, 0)

    def drain(i, _):
        _, valid, thead = target(i)

        @pl.when(valid)
        def _():
            kv_copy(i).wait_send()
            remote(q_stage.at[thead], block(qbuf, chip, ROWS), qsend.at[thead], qrecv.at[0],
                   sibling).wait_send()
            list_copy(i).wait_send()

        return 0

    lax.fori_loop(1, CHIPS, drain, 0)

    @pl.when(has_head)
    def _():
        def drain_head(src, _):
            forward(src).wait_send()

            @pl.when(src != chip)
            def _():
                part = block(obuf, src, ROWS)
                remote(part, part, osend.at[src], orecv_sem.at[0], sibling).wait_send()

            return 0

        lax.fori_loop(0, CHIPS, drain_head, 0)


def restore(order_ref, rows_ref, out_ref, perm):
    @pl.when(pl.program_id(0) == 0)
    def _():
        perm[...] = (
            lax.broadcasted_iota(jnp.int32, (ROWS, ROWS), 0) == order_ref[...]
        ).astype(jnp.bfloat16)

    out_ref[...] = jnp.dot(perm[...], rows_ref[...],
                           preferred_element_type=jnp.float32).astype(jnp.bfloat16)


def body(tokens, queries, keyvals, out_weight, gate, cube_order, crit_owner, crit_tile, crit_count):
    live = jnp.arange(LIST, dtype=jnp.int32)[None, :] < crit_count[0][:, None]
    k_at = crit_owner[0] * (2 * QT) + crit_tile[0]
    v_at = jnp.where(live, k_at + QT, KV_TILES)
    m_at = jnp.where(live, 0, 1)

    def wide(part):
        return jnp.pad(part, ((0, 0), (0, 16 - LIST)))

    codes = jnp.concatenate([wide(k_at), wide(v_at), wide(m_at)], axis=1)
    codes = jnp.pad(codes, ((0, 0), (0, 128 - codes.shape[1])))
    bf16, i32 = jnp.bfloat16, jnp.int32
    dma = pltpu.SemaphoreType.DMA
    rows, order = pl.pallas_call(
        kernel,
        out_shape=(
            jax.ShapeDtypeStruct((ROWS, D), bf16),
            jax.ShapeDtypeStruct((1, ROWS), i32),
        ),
        in_specs=[pl.BlockSpec(memory_space=pl.ANY)] * 4
        + [pl.BlockSpec(memory_space=pltpu.VMEM)] * 3,
        out_specs=(
            pl.BlockSpec(memory_space=pl.ANY),
            pl.BlockSpec(memory_space=pl.ANY),
        ),
        scratch_shapes=[
            pltpu.VMEM((ROWS, D), bf16),
            pltpu.VMEM((ROWS, HW), bf16),
            pltpu.VMEM((ROWS, 2, HW), bf16),
            pltpu.VMEM((HW, D), bf16),
            pltpu.VMEM((ROWS, ROWS), bf16),
            pltpu.VMEM((ROWS, D), bf16),
            pltpu.VMEM((HEADS, 2 * QT, TILE, HEAD_DIM), bf16),
            pltpu.VMEM((HEADS, ROWS, HEAD_DIM), bf16),
            pltpu.VMEM((KV_TILES + 1, TILE, HEAD_DIM), bf16),
            pltpu.VMEM((CHIPS * ROWS, HEAD_DIM), bf16),
            pltpu.VMEM((CHIPS * ROWS, HEAD_DIM), bf16),
            pltpu.VMEM((2, TILE, HEAD_DIM), bf16),
            pltpu.VMEM((CHIPS * QT, 128), i32),
            pltpu.SMEM((CHIPS * QT, 128), i32),
            pltpu.VMEM((HEADS, ROWS, HEAD_DIM), bf16),
            pltpu.VMEM((ROWS, D), bf16),
            pltpu.VMEM((2, ROWS, D - Y_COLS), bf16),
            dma((4,)), dma, dma((HEADS,)), dma((CHIPS,)), dma((CHIPS,)), dma((CHIPS,)),
            dma((HEADS,)), dma((CHIPS * NCH,)), dma((HEADS,)), dma((CHIPS,)),
            dma((CHIPS,)), dma((QT * HEADS,)), dma((AHEAD, NCH)), dma((AHEAD, NCH)), dma((3, NCH)), dma((3, NCH)),
            dma, dma,
        ],
        compiler_params=pltpu.CompilerParams(
            collective_id=0, has_side_effects=True, vmem_limit_bytes=60 * 2**20
        ),
        cost_estimate=pl.CostEstimate(
            flops=16 * 10**9, bytes_accessed=22 * 2**20, transcendentals=10**7
        ),
        name="cube_attention",
    )(tokens[0], queries[0], keyvals[0], out_weight[0], gate, cube_order[0], codes)
    handed = pl.pallas_call(
        restore,
        out_shape=jax.ShapeDtypeStruct((ROWS, D), bf16),
        grid=(D // R_COLS,),
        in_specs=[
            pl.BlockSpec((1, ROWS), lambda n: (0, 0)),
            pl.BlockSpec((ROWS, R_COLS), lambda n: (0, n)),
        ],
        out_specs=pl.BlockSpec((ROWS, R_COLS), lambda n: (0, n)),
        scratch_shapes=[pltpu.VMEM((ROWS, ROWS), bf16)],
        name="token_order",
    )(order, rows)
    return handed[None]


def solution(mesh):
    in_specs = (
        P("section", "ctx", None),
        P("section", "ctx", None),
        P("section", "ctx", None, None),
        P("section", None, None),
        P("section", None),
        P("section", "ctx", None),
        P("section", "ctx", None),
        P("section", "ctx", None),
        P("section", "ctx"),
    )
    out_specs = P("section", "ctx", None)
    return jax.shard_map(body, mesh=mesh, in_specs=in_specs, out_specs=out_specs, check_vma=False)
```

```python
import math

import jax
import jax.numpy as jnp
from jax import lax
from jax.experimental import pallas as pl
from jax.experimental.pallas import tpu as pltpu
from jax.sharding import PartitionSpec as P

D = 3072
HEADS = 12
HEAD_DIM = 128
TILE = 64
LIST = 12
QT = 8
HW = 1536
ROWS = 512
CTX = 32
SIDE = 4
CHIPS = 16
SECTIONS = 4
KV_TILES = CTX * 2 * QT
JT = 1
CHUNK = JT * TILE
NCH = QT // JT
UNROLL = 8
Q_FIRST = 1
LAG = 1
HOP = 2
Y_COLS = 2304
P_COLS = D - Y_COLS
AHEAD = Y_COLS // P_COLS
ROUND = 8
NCOL = 512
R_COLS = 1024
EXP_SCALE = math.log2(math.e) / math.sqrt(HEAD_DIM)


def kernel(
    tok_hbm, q_hbm, kv_hbm, w_hbm, gate_ref, order_ref, codes_ref, yrecv, prev_order,
    tok, q_in, kv_in, w, perm, tok_cube, kv_stage, q_stage, kvbuf, qbuf, obuf, ones,
    lists, lists_smem, orecv, ystage, relay,
    load_sem, smem_sem, ksend, krecv, fsend, frecv, qsend, qrecv, lsend, lrecv,
    osend, orecv_sem, ysend, yrecv_sem, bsend, brecv, psend, precv,
):
    sec = lax.axis_index("section")
    me = lax.axis_index("ctx")
    core = me % 2
    chip = me // 2
    cx, cz = chip // SIDE, chip % SIDE
    kind = (cz - cx + 3) % SIDE
    has_head = kind < 3
    head = cx + SIDE * kind
    sibling = (sec, me + 1 - 2 * core)
    ahead = ((sec + 1) % SECTIONS, me)
    behind = ((sec + SECTIONS - 1) % SECTIONS, me)

    def remote(src, dst, send, recv, device):
        return pltpu.make_async_remote_copy(
            src_ref=src, dst_ref=dst, send_sem=send, recv_sem=recv,
            device_id=device, device_id_type=pl.DeviceIdType.MESH,
        )

    def load(i):
        src = (kv_hbm, q_hbm, tok_hbm, w_hbm)[i]
        return pltpu.make_async_copy(src, (kv_in, q_in, tok, w)[i], load_sem.at[i])

    load(0).start()

    barrier = pltpu.get_barrier_semaphore()

    def greet(i, _):
        other = (chip + i) % CHIPS
        pl.semaphore_signal(barrier, inc=1, device_id=(sec, 2 * other + core),
                            device_id_type=pl.DeviceIdType.MESH)
        return 0

    lax.fori_loop(1, CHIPS, greet, 0)
    for device in (sibling, ahead, behind):
        pl.semaphore_signal(barrier, inc=1, device_id=device,
                            device_id_type=pl.DeviceIdType.MESH)

    column = jnp.transpose(jnp.broadcast_to(order_ref[...], (128, ROWS)))[:, :1]
    perm[...] = (lax.broadcasted_iota(jnp.int32, (ROWS, ROWS), 1) == column).astype(jnp.bfloat16)
    ones[0] = jnp.ones((TILE, HEAD_DIM), jnp.bfloat16)
    ones[1] = jnp.zeros((TILE, HEAD_DIM), jnp.bfloat16)
    kvbuf[KV_TILES] = jnp.zeros((TILE, HEAD_DIM), jnp.bfloat16)

    pl.semaphore_wait(barrier, CHIPS + 2)

    def order_copy():
        return remote(order_ref, prev_order, psend, precv, ahead)

    order_copy().start()

    def shift(i):
        dx, dz = i % SIDE, (i // SIDE + 3 * (i % SIDE)) % SIDE
        return dx + core * (dz - dx), dz + core * (dx - dz)

    def target(i):
        dx, dz = shift(i)
        tx, tz = (cx + dx) % SIDE, (cz + dz) % SIDE
        tkind = (tz - tx + 3) % SIDE
        return tx * SIDE + tz, tkind < 3, tx + SIDE * tkind

    def origin(i):
        dx, dz = shift(i)
        return ((cx + SIDE - dx) % SIDE) * SIDE + (cz + SIDE - dz) % SIDE

    def block(ref, index, rows):
        return ref.at[pl.ds(pl.multiple_of(index * rows, rows), rows)]

    def list_copy(i):
        to, _, thead = target(i)
        return remote(codes_ref, block(lists, chip, QT), lsend.at[thead], lrecv.at[chip],
                      (sec, 2 * to + core))

    def kv_copy(i):
        to, _, thead = target(i)
        return remote(kv_stage.at[thead], block(kvbuf, me, 2 * QT), ksend.at[thead],
                      krecv.at[chip], (sec, 2 * to + core))

    def q_rows(src, ch):
        return pl.ds(pl.multiple_of(src * ROWS + ch * CHUNK, CHUNK), CHUNK)

    def q_copy(i, ch):
        to, _, thead = target(i)
        rows = pl.ds(pl.multiple_of(ch * CHUNK, CHUNK), CHUNK)
        return remote(q_stage.at[thead, rows], qbuf.at[q_rows(chip, ch)], qsend.at[thead],
                      qrecv.at[chip * NCH + ch], (sec, 2 * to + core))

    def forward(from_chip):
        part = block(kvbuf, 2 * from_chip + core, 2 * QT)
        return remote(part, part, fsend.at[from_chip], frecv.at[from_chip], sibling)

    def lanes(h):
        return pl.ds(pl.multiple_of(h * HEAD_DIM, HEAD_DIM), HEAD_DIM)

    def cube_pairs(h):
        both = jnp.concatenate([kv_in[:, 0, lanes(h)], kv_in[:, 1, lanes(h)]], axis=1)
        rows = jnp.dot(perm[...], both, preferred_element_type=jnp.float32).astype(jnp.bfloat16)
        rows = rows.reshape(QT, TILE, 2 * HEAD_DIM)
        return rows[:, :, :HEAD_DIM], rows[:, :, HEAD_DIM:]

    def cube_query(h):
        return jnp.dot(perm[...], q_in[:, lanes(h)],
                       preferred_element_type=jnp.float32).astype(jnp.bfloat16)

    load(0).wait()
    for i in range(1, 4):
        load(i).start()

    def send_kv(i, _):
        _, valid, thead = target(i)

        @pl.when(valid)
        def _():
            keys, values = cube_pairs(thead)
            kv_stage[thead, 0:QT] = keys
            kv_stage[thead, QT:] = values
            kv_copy(i).start()
            list_copy(i).start()

        return 0

    lax.fori_loop(1, CHIPS, send_kv, 0)

    @pl.when(has_head)
    def _():
        keys, values = cube_pairs(head)
        kvbuf[pl.ds(me * 2 * QT, QT)] = keys
        kvbuf[pl.ds(me * 2 * QT + QT, QT)] = values
        forward(chip).start()
        lists[pl.ds(pl.multiple_of(chip * QT, QT), QT)] = codes_ref[...]

    load(1).wait()

    def make_q(i, _):
        _, valid, thead = target(i)

        @pl.when(valid)
        def _():
            q_stage[thead] = cube_query(thead)

        return 0

    lax.fori_loop(1, CHIPS, make_q, 0)

    def send_q(ch):
        def one(i, _):
            _, valid, _ = target(i)

            @pl.when(valid)
            def _():
                q_copy(i, ch).start()

            return 0

        lax.fori_loop(1, CHIPS, one, 0)

    for ch in range(Q_FIRST):
        send_q(ch)

    @pl.when(has_head)
    def _():
        qbuf[pl.ds(pl.multiple_of(chip * ROWS, ROWS), ROWS)] = cube_query(head)

    load(2).wait()

    def cube_tokens(n, _):
        cols = pl.ds(pl.multiple_of(n * NCOL, NCOL), NCOL)
        tok_cube[:, cols] = jnp.dot(perm[...], tok[:, cols],
                                    preferred_element_type=jnp.float32).astype(jnp.bfloat16)
        return 0

    lax.fori_loop(0, D // NCOL, cube_tokens, 0)

    @pl.when(has_head)
    def _():
        def pass_on(i, _):
            src = origin(i)
            remote(kv_stage.at[0], block(kvbuf, 2 * src + core, 2 * QT), ksend.at[0],
                   krecv.at[src], sibling).wait_recv()
            forward(src).start()
            return 0

        lax.fori_loop(1, CHIPS, pass_on, 0)

        def small(i, _):
            src = origin(i)
            remote(codes_ref, block(lists, src, QT), lsend.at[0], lrecv.at[src],
                   sibling).wait_recv()
            return 0

        lax.fori_loop(1, CHIPS, small, 0)

        to_smem = pltpu.make_async_copy(lists, lists_smem, smem_sem)
        to_smem.start()

        def passed(src, _):
            part = block(kvbuf, 2 * src + 1 - core, 2 * QT)
            remote(part, part, fsend.at[src], frecv.at[src], sibling).wait_recv()
            return 0

        lax.fori_loop(0, CHIPS, passed, 0)
        to_smem.wait()

    load(3).wait()

    def o_rows(src, j):
        return pl.ds(pl.multiple_of(src * ROWS + j * TILE, TILE), TILE)

    def attend(src, j):
        q = qbuf[o_rows(src, j), :]
        row = src * QT + j
        ks, vs, marks = [], [], []
        for e in range(LIST):
            ks.append(kvbuf[lists_smem[row, e]])
            vs.append(kvbuf[lists_smem[row, 16 + e]])
            marks.append(ones[lists_smem[row, 32 + e]])
        scores = lax.dot_general(q, jnp.concatenate(ks, 0), (((1,), (1,)), ((), ())),
                                 preferred_element_type=jnp.float32)
        top = jnp.max(scores, axis=-1, keepdims=True)
        weights = jnp.exp2((scores - top) * EXP_SCALE).astype(jnp.bfloat16)
        sums = jnp.concatenate([jnp.concatenate(vs, 0), jnp.concatenate(marks, 0)], 1)
        both = jnp.dot(weights, sums, preferred_element_type=jnp.float32)
        obuf[o_rows(src, j), :] = (both[:, :HEAD_DIM] / both[:, HEAD_DIM:]).astype(jnp.bfloat16)

    def send_o(src, j):
        part = obuf.at[o_rows(src, j)]
        place = orecv.at[head, pl.ds(pl.multiple_of(j * TILE, TILE), TILE)]
        sem = orecv_sem.at[j * HEADS + head]

        @pl.when(src != chip)
        def _():
            remote(part, place, osend.at[src], sem, (sec, 2 * src + core)).start()

        @pl.when(src == chip)
        def _():
            pltpu.make_async_copy(part, place, sem).start()

    def y_copy(ch, n):
        rows = pl.ds(pl.multiple_of(ch * CHUNK, CHUNK), CHUNK)
        cols = pl.ds(pl.multiple_of(n * P_COLS, P_COLS), P_COLS)
        return remote(ystage.at[rows, cols], yrecv.at[rows, cols], ysend.at[n, ch],
                      yrecv_sem.at[n, ch], ahead)

    def rest_copy(ch):
        rows = pl.ds(pl.multiple_of(ch * CHUNK, CHUNK), CHUNK)
        cols = pl.ds(Y_COLS, D - Y_COLS)
        return remote(ystage.at[rows, cols], yrecv.at[rows, cols], bsend.at[0, ch],
                      brecv.at[2, ch], ahead)

    def back_copy(hop, ch):
        rows = pl.ds(pl.multiple_of(ch * CHUNK, CHUNK), CHUNK)
        cols = pl.ds(Y_COLS, D - Y_COLS)
        if hop == 0:
            src, dst = ystage.at[rows, cols], relay.at[0, rows]
        elif hop == 1:
            src, dst = relay.at[0, rows], relay.at[1, rows]
        else:
            src, dst = relay.at[1, rows], yrecv.at[rows, cols]
        return remote(src, dst, bsend.at[hop, ch], brecv.at[hop, ch], behind)

    def q_wait(src, ch):
        @pl.when(src != chip)
        def _():
            remote(q_stage.at[0, pl.ds(0, CHUNK)], qbuf.at[q_rows(src, ch)], qsend.at[0],
                   qrecv.at[src * NCH + ch], sibling).wait_recv()

    def chunk_step(ch, _):
        @pl.when(ch + Q_FIRST < NCH)
        def _():
            send_q(ch + Q_FIRST)

        for hop in (2, 1):
            moved = ch - LAG - HOP * hop

            @pl.when((moved >= 0) & (moved < ROUND))
            def _():
                back_copy(hop - 1, moved).wait_recv()
                back_copy(hop, moved).start()

        @pl.when(has_head & (ch < NCH))
        def _():
            def group(g, _):
                j = ch * JT + g // (CHIPS // UNROLL)
                first = (g % (CHIPS // UNROLL)) * UNROLL
                sources = [origin((first + u + 1) % CHIPS) for u in range(UNROLL)]

                @pl.when(j == ch * JT)
                def _():
                    for src in sources:
                        q_wait(src, ch)

                for src in sources:
                    attend(src, j)
                for src in sources:
                    send_o(src, j)
                return 0

            lax.fori_loop(0, JT * CHIPS // UNROLL, group, 0)

        @pl.when((ch >= LAG) & (ch < NCH + LAG))
        def _():
            done = ch - LAG

            def arrived(k, _):
                j = done * JT + k // HEADS
                h = k % HEADS
                place = orecv.at[h, pl.ds(pl.multiple_of(j * TILE, TILE), TILE)]
                pltpu.make_async_copy(obuf.at[pl.ds(0, TILE)], place,
                                      orecv_sem.at[j * HEADS + h]).wait()
                return 0

            lax.fori_loop(0, JT * HEADS, arrived, 0)
            rows = pl.ds(pl.multiple_of(done * CHUNK, CHUNK), CHUNK)
            attended = jnp.concatenate([orecv[h, rows, :] for h in range(HEADS)], axis=1)

            def project(k, _):
                n = (k + AHEAD) % (AHEAD + 1)
                cols = pl.ds(pl.multiple_of(n * P_COLS, P_COLS), P_COLS)
                acc = jnp.dot(attended, w[:, cols], preferred_element_type=jnp.float32)
                ystage[rows, cols] = (
                    tok_cube[rows, cols].astype(jnp.float32) + gate_ref[0:1, cols] * acc
                ).astype(jnp.bfloat16)

                @pl.when((k == 0) & (done < ROUND))
                def _():
                    back_copy(0, done).start()

                @pl.when((k == 0) & (done >= ROUND))
                def _():
                    rest_copy(done).start()

                @pl.when(k > 0)
                def _():
                    y_copy(done, n).start()

                return 0

            lax.fori_loop(0, AHEAD + 1, project, 0)

        return 0

    lax.fori_loop(0, max(NCH + LAG, ROUND + LAG + 2 * HOP), chunk_step, 0)

    order_copy().wait()

    def y_wait(ch, _):
        for n in range(AHEAD):
            y_copy(ch, n).wait()
        rest_copy(ch).wait()

        @pl.when(ch < ROUND)
        def _():
            back_copy(1, ch).wait_send()
            back_copy(2, ch).wait_send()

        return 0

    lax.fori_loop(0, NCH, y_wait, 0)

    def drain(i, _):
        _, valid, thead = target(i)

        @pl.when(valid)
        def _():
            kv_copy(i).wait_send()
            remote(q_stage.at[thead], block(qbuf, chip, ROWS), qsend.at[thead], qrecv.at[0],
                   sibling).wait_send()
            list_copy(i).wait_send()

        return 0

    lax.fori_loop(1, CHIPS, drain, 0)

    @pl.when(has_head)
    def _():
        def drain_head(src, _):
            forward(src).wait_send()

            @pl.when(src != chip)
            def _():
                part = block(obuf, src, ROWS)
                remote(part, part, osend.at[src], orecv_sem.at[0], sibling).wait_send()

            return 0

        lax.fori_loop(0, CHIPS, drain_head, 0)


def restore(order_ref, rows_ref, out_ref, perm):
    @pl.when(pl.program_id(0) == 0)
    def _():
        perm[...] = (
            lax.broadcasted_iota(jnp.int32, (ROWS, ROWS), 0) == order_ref[...]
        ).astype(jnp.bfloat16)

    out_ref[...] = jnp.dot(perm[...], rows_ref[...],
                           preferred_element_type=jnp.float32).astype(jnp.bfloat16)


def body(tokens, queries, keyvals, out_weight, gate, cube_order, crit_owner, crit_tile, crit_count):
    live = jnp.arange(LIST, dtype=jnp.int32)[None, :] < crit_count[0][:, None]
    k_at = crit_owner[0] * (2 * QT) + crit_tile[0]
    v_at = jnp.where(live, k_at + QT, KV_TILES)
    m_at = jnp.where(live, 0, 1)

    def wide(part):
        return jnp.pad(part, ((0, 0), (0, 16 - LIST)))

    codes = jnp.concatenate([wide(k_at), wide(v_at), wide(m_at)], axis=1)
    codes = jnp.pad(codes, ((0, 0), (0, 128 - codes.shape[1])))
    bf16, i32 = jnp.bfloat16, jnp.int32
    dma = pltpu.SemaphoreType.DMA
    rows, order = pl.pallas_call(
        kernel,
        out_shape=(
            jax.ShapeDtypeStruct((ROWS, D), bf16),
            jax.ShapeDtypeStruct((1, ROWS), i32),
        ),
        in_specs=[pl.BlockSpec(memory_space=pl.ANY)] * 4
        + [pl.BlockSpec(memory_space=pltpu.VMEM)] * 3,
        out_specs=(
            pl.BlockSpec(memory_space=pl.ANY),
            pl.BlockSpec(memory_space=pl.ANY),
        ),
        scratch_shapes=[
            pltpu.VMEM((ROWS, D), bf16),
            pltpu.VMEM((ROWS, HW), bf16),
            pltpu.VMEM((ROWS, 2, HW), bf16),
            pltpu.VMEM((HW, D), bf16),
            pltpu.VMEM((ROWS, ROWS), bf16),
            pltpu.VMEM((ROWS, D), bf16),
            pltpu.VMEM((HEADS, 2 * QT, TILE, HEAD_DIM), bf16),
            pltpu.VMEM((HEADS, ROWS, HEAD_DIM), bf16),
            pltpu.VMEM((KV_TILES + 1, TILE, HEAD_DIM), bf16),
            pltpu.VMEM((CHIPS * ROWS, HEAD_DIM), bf16),
            pltpu.VMEM((CHIPS * ROWS, HEAD_DIM), bf16),
            pltpu.VMEM((2, TILE, HEAD_DIM), bf16),
            pltpu.VMEM((CHIPS * QT, 128), i32),
            pltpu.SMEM((CHIPS * QT, 128), i32),
            pltpu.VMEM((HEADS, ROWS, HEAD_DIM), bf16),
            pltpu.VMEM((ROWS, D), bf16),
            pltpu.VMEM((2, ROWS, D - Y_COLS), bf16),
            dma((4,)), dma, dma((HEADS,)), dma((CHIPS,)), dma((CHIPS,)), dma((CHIPS,)),
            dma((HEADS,)), dma((CHIPS * NCH,)), dma((HEADS,)), dma((CHIPS,)),
            dma((CHIPS,)), dma((QT * HEADS,)), dma((AHEAD, NCH)), dma((AHEAD, NCH)), dma((3, NCH)), dma((3, NCH)),
            dma, dma,
        ],
        compiler_params=pltpu.CompilerParams(
            collective_id=0, has_side_effects=True, vmem_limit_bytes=60 * 2**20
        ),
        cost_estimate=pl.CostEstimate(
            flops=16 * 10**9, bytes_accessed=22 * 2**20, transcendentals=10**7
        ),
        name="cube_attention",
    )(tokens[0], queries[0], keyvals[0], out_weight[0], gate, cube_order[0], codes)
    handed = pl.pallas_call(
        restore,
        out_shape=jax.ShapeDtypeStruct((ROWS, D), bf16),
        grid=(D // R_COLS,),
        in_specs=[
            pl.BlockSpec((1, ROWS), lambda n: (0, 0)),
            pl.BlockSpec((ROWS, R_COLS), lambda n: (0, n)),
        ],
        out_specs=pl.BlockSpec((ROWS, R_COLS), lambda n: (0, n)),
        scratch_shapes=[pltpu.VMEM((ROWS, ROWS), bf16)],
        name="token_order",
    )(order, rows)
    return handed[None]


def solution(mesh):
    in_specs = (
        P("section", "ctx", None),
        P("section", "ctx", None),
        P("section", "ctx", None, None),
        P("section", None, None),
        P("section", None),
        P("section", "ctx", None),
        P("section", "ctx", None),
        P("section", "ctx", None),
        P("section", "ctx"),
    )
    out_specs = P("section", "ctx", None)
    return jax.shard_map(body, mesh=mesh, in_specs=in_specs, out_specs=out_specs, check_vma=False)
```
